32 devices in a mesh: expert: 8 (over z, x), shard: 4 (over y, core).
Axes of the slice: x: 2, y: 2, z: 4, core: 2. Of those that a mesh axis runs over, the one named last changes fastest.
Arguments:
- tokens: bfloat16 [2048, 768], P('expert', 'shard'), may hold values from -6 to 6
- norm_gain1: float32 [768], replicated, may hold values from 0.5 to 1.5
- qkv_weight: bfloat16 [768, 2304], P(None, 'shard'), may hold values from -0.21875 to 0.21875
- out_weight: bfloat16 [768, 768], P('shard'), may hold values from -0.625 to 0.625
- rel_bias: float32 [12, 32], P('shard'), may hold values from -4 to 4
- norm_gain2: float32 [768], replicated, may hold values from 0.5 to 1.5
- router_weight: bfloat16 [768, 8], replicated, may hold values from -0.15625 to 0.15625
- in_weight: bfloat16 [8, 768, 3072], P('expert', None, 'shard'), may hold values from -0.21875 to 0.21875
- expert_out: bfloat16 [8, 3072, 768], P('expert', 'shard'), may hold values from -0.109375 to 0.109375
- lengths: int32 [8], P('expert'), may hold values from 32 to 256, as said below
- routes: int32 [2048, 2], P('expert'), may hold values from 0 to 7, all different within a row; in each aligned block of 256 rows (0 to 255, 256 to 511, ...) at most 96 rows name the same one
- cotangent: bfloat16 [2048, 768], P('expert', 'shard'), may hold values from -6 to 6
Outputs:
- output: bfloat16 [2048, 768], P('expert', 'shard')
- grad_tokens: float32 [2048, 768], P('expert', 'shard')
- grad_gain1: float32 [768], replicated
- grad_qkv: float32 [768, 2304], P(None, 'shard')
- grad_out_weight: float32 [768, 768], P('shard')
- grad_rel_bias: float32 [12, 32], P('shard')
- grad_gain2: float32 [768], replicated
- grad_router: float32 [768, 8], replicated
- grad_in_weight: float32 [8, 768, 3072], P('expert', None, 'shard')
- grad_expert_out: float32 [8, 3072, 768], P('expert', 'shard')
The draws below stay inside these ranges and needn't reach their ends.
Inputs may be any that keep to these rules, and one draw needn't show every extreme that they name: A sequence holds its 256 slots on one index of the expert axis; lengths of at least 32, and some sequence uses all 256. `routes`: the two experts of a slot differ; among the 256 slots of one sequence no expert is named more than 96 times, a bound that some block reaches.
All inputs are finite; a program needn't handle non-finite values.
Results may differ from the reference program's by a relative error of at most 0.015.
Values may be sent and summed in bfloat16 or wider, within the bound.
A program may use at most 128 MiB of HBM per device.

```python
import math
import jax
import jax.numpy as jnp
import numpy as np
from jax import lax

D = 768
HEADS = 12
HD = 64
FF = 3072
TOP = 2
BUCKETS = 32
MAX_DIST = 128
TOK_DEV = 256
EXPERTS = 8
SEQS = 8
TOKENS = 2048
CAP = 96
N_EXPERT = 8
N_SHARD = 4


def draw_lengths(key, part):
    key = jax.random.fold_in(key, 7)
    first_key, second_key = jax.random.split(key)
    drawn = jax.random.randint(first_key, (SEQS,), TOK_DEV // 8, TOK_DEV + 1)
    longest = jax.random.randint(second_key, (), 0, SEQS)
    return jnp.where(jnp.arange(SEQS) == longest, TOK_DEV, drawn).astype(jnp.int32)


def block_scale(rng, dims, pieces, smallest, high):
    level, own = 1.0, jax.random.fold_in(rng, 6)
    for position, shards_of in pieces:
        heights = jnp.exp(jax.random.uniform(jax.random.fold_in(own, position), (shards_of,), jnp.float32, smallest / len(pieces), high / len(pieces)))
        level = level * jnp.repeat(heights, dims[position] // shards_of).reshape([-1 if axis == position else 1 for axis in range(len(dims))])
    return level


def shared_out(stream_key, own, number, rows, amount, top, limit, slope):
    ranking = jax.random.permutation(stream_key, amount)
    heavy_load, usual = shares(amount, rows * top, limit, slope, True), shares(amount, rows * top, limit, slope, False)
    places = jnp.arange(amount)

    def named(sizes, rotation):
        used = int((sizes > 0).sum())
        fixed = max(1, used // 4)
        shifted = fixed + (places - fixed + rotation * (used - fixed)) % max(1, amount - fixed)
        return jnp.zeros((amount,), jnp.int32).at[ranking[jnp.where(places < fixed, places, shifted)]].set(jnp.asarray(sizes, jnp.int32))

    sizes = jnp.where(number % 4 == 0, named(heavy_load, number // 4), named(usual, number - number // 4 - 1))
    mixed = jax.random.permutation(jax.random.fold_in(own, 3), amount)
    giver, receiver = mixed[0:amount // 2 * 2:2], mixed[1:amount // 2 * 2:2]
    margin = jnp.minimum(sizes[giver] - 1, limit - sizes[receiver]) // 2
    margin = jnp.where((giver == ranking[0]) | (receiver == ranking[0]) | (sizes[receiver] == 0), 0, jnp.maximum(margin, 0))
    shifted = jax.random.randint(jax.random.fold_in(own, 4), (amount // 2,), 0, 1 << 20) % (margin + 1)
    sizes = sizes.at[giver].add(-shifted).at[receiver].add(shifted)
    members = jnp.searchsorted(jnp.cumsum(sizes), jnp.arange(rows * top), side="right").astype(jnp.int32)
    grid = members.reshape(top, rows).T
    grid = grid[jax.random.permutation(jax.random.fold_in(own, 1), rows)]
    rotation = jax.random.randint(jax.random.fold_in(own, 2), (rows, 1), 0, top)
    return jnp.take_along_axis(grid, (jnp.arange(top)[None, :] + rotation) % top, axis=1)


def shares(count, total, bound, slope, full):
    loads = [(1 << 20) // math.isqrt(grade ** slope) + 1 for grade in range(1, count + 1)]
    largest = bound if full else min(bound, max(-(-total // count), total * loads[0] // sum(loads)))
    least = 1 if total - largest >= count - 1 else 0
    given, spare = [largest] + [least] * (count - 1), total - largest - least * (count - 1)
    while spare > 0:
        candidates = [i for i in range(1, count) if given[i] < largest] or [i for i in range(1, count) if given[i] < bound]
        pool, left = sum([loads[i] for i in candidates]), spare
        for i in candidates:
            addition = min(bound - given[i], max(1, left * loads[i] // pool), spare)
            given[i] = given[i] + addition
            spare = spare - addition
    return np.array(given)


def scatter_about(rng, shape, scale, most, cuts=(), held_as=jnp.bfloat16):
    values = jax.random.normal(rng, shape, jnp.float32) * scale
    if len(cuts) > 0:
        values = block_scale(rng, shape, cuts, -0.22, 0.18) * values
    return jnp.clip(values, min=-most, max=most).astype(held_as)


def setup_inputs(seed: int = 0) -> dict:
    key_of = jax.random.split(jax.random.key(seed), 13)
    tokens = scatter_about(key_of[0], (TOKENS, D), 1.0, 6.0, ((0, 8), (1, 4)))
    norm_gain1 = jnp.clip(1.0 + 0.1 * jax.random.normal(key_of[1], (D,), jnp.float32), 0.5, 1.5)
    qkv_weight = scatter_about(key_of[2], (D, 3 * D), D ** -0.5, 0.21875, ((1, 4),))
    out_weight = scatter_about(key_of[3], (D, D), (D // 8) ** -0.5, 0.625, ((0, 4),))
    rel_bias = scatter_about(key_of[4], (HEADS, BUCKETS), 1.0, 4.0, ((0, 4),), jnp.float32)
    norm_gain2 = jnp.clip(1.0 + 0.1 * jax.random.normal(key_of[5], (D,), jnp.float32), 0.5, 1.5)
    router_weight = scatter_about(key_of[6], (D, EXPERTS), (2 * D) ** -0.5, 0.15625)
    in_weight = scatter_about(key_of[7], (EXPERTS, D, FF), D ** -0.5, 0.21875, ((0, 8), (2, 4)))
    expert_out = scatter_about(key_of[8], (EXPERTS, FF, D), FF ** -0.5, 0.109375, ((0, 8), (1, 4)))
    lengths = draw_lengths(jax.random.fold_in(key_of[12], 71), 0)
    routes_keys = jax.random.split(jax.random.fold_in(key_of[10], 1), TOKENS // TOK_DEV)
    routes_turns = jax.random.permutation(jax.random.fold_in(key_of[10], 3), TOKENS // TOK_DEV)
    routes = jax.vmap(lambda own, number: shared_out(jax.random.fold_in(key_of[10], 2), own, number, TOK_DEV, EXPERTS, TOP, CAP, 2))(routes_keys, routes_turns).reshape((TOKENS, TOP))
    cotangent = scatter_about(key_of[11], (TOKENS, D), 1.0, 6.0, ((0, 8), (1, 4)))
    return {"tokens": tokens, "norm_gain1": norm_gain1, "qkv_weight": qkv_weight, "out_weight": out_weight, "rel_bias": rel_bias, "norm_gain2": norm_gain2, "router_weight": router_weight, "in_weight": in_weight, "expert_out": expert_out, "lengths": lengths, "routes": routes, "cotangent": cotangent}


@jax.custom_vjp
def low(v):
    return lax.optimization_barrier(v.astype(jnp.bfloat16)).astype(jnp.float32)

@jax.custom_vjp
def low_back(v):
    return v

def low_keep(v):
    return (low(v), None)

def low_pass(kept, grad):
    return (grad,)

def back_keep(v):
    return (v, None)

def back_low(kept, grad):
    return (low(grad),)
low.defvjp(low_keep, low_pass)
low_back.defvjp(back_keep, back_low)
HIGH = lax.Precision.HIGHEST
EPSILON = 1e-06

def bucket_of(distance):
    half = BUCKETS // 2
    powers = np.arange(1, half)
    edges = np.ceil(half * (MAX_DIST / half) ** (powers / half))
    counted = jnp.zeros(distance.shape, jnp.int32)
    for threshold in edges:
        counted = counted + (distance >= int(threshold)).astype(jnp.int32)
    return jnp.where(distance < half, distance, half + counted)

def normed(values, gain):
    return values * lax.rsqrt(lax.optimization_barrier(jnp.mean(values * values, axis=-1, keepdims=True)) + EPSILON) * gain

def gates_of(logits, routes):
    probability = jax.nn.softmax(logits, axis=-1)
    chosen = routes[:, :, None] == jnp.arange(logits.shape[1])[None, None, :]
    picked = lax.optimization_barrier(jnp.sum(jnp.where(chosen, probability[:, None, :], 0.0), axis=2))
    return picked / lax.optimization_barrier(jnp.sum(picked, axis=1, keepdims=True))

def attend(normal_in, seq_length, w_query, w_key, w_value, w_output, table_in):
    span = normal_in.shape[0]

    def heads_of(weight):
        return low(low_back(jnp.dot(normal_in, weight, precision=HIGH))).reshape(span, HEADS, HD)
    queries = heads_of(w_query)
    keys_low = heads_of(w_key)
    values_low = heads_of(w_value)
    positions = jnp.arange(span)
    distance = positions[:, None] - positions[None, :]
    allowed = (distance >= 0) & (positions[None, :] < seq_length)
    bias_mat = table_in[:, bucket_of(jnp.maximum(distance, 0))]
    scores = jnp.einsum('ihd,jhd->hij', queries, keys_low, precision=HIGH) * HD ** (-0.5) + bias_mat
    scores = low_back(jnp.where(allowed[None], scores, -1000000000.0))
    weights = low(jax.nn.softmax(scores, axis=-1))
    attended = jnp.einsum('hij,jhd->ihd', weights, values_low, precision=HIGH).reshape(span, D)
    attended = low_back(low(attended))
    validity = (positions < seq_length).astype(jnp.float32)
    return low_back(jnp.dot(attended, w_output, precision=HIGH)) * validity[:, None]

def reference(tokens, norm_gain1, qkv_weight, out_weight, rel_bias, norm_gain2, router_weight, in_weight, expert_out, lengths, routes, cotangent):
    token_ids = jnp.arange(TOKENS, dtype=jnp.int32)
    valid = (token_ids % TOK_DEV < lengths[token_ids // TOK_DEV]).astype(jnp.float32)
    flat_expert = routes.reshape(-1)
    one_hot = (flat_expert[:, None] == jnp.arange(EXPERTS, dtype=jnp.int32)[None, :]).astype(jnp.int32)
    one_hot = one_hot.reshape(N_EXPERT, TOK_DEV * TOP, EXPERTS)
    ranks = (lax.optimization_barrier(jnp.sum(jnp.cumsum(one_hot, axis=1) * one_hot, axis=2)) - 1).reshape(-1)
    source = jnp.arange(TOKENS * TOP, dtype=jnp.int32) // (TOK_DEV * TOP)
    slot_index = (source * CAP + ranks).astype(jnp.int32)
    slot_token = jnp.full((EXPERTS, N_EXPERT * CAP), TOKENS, jnp.int32)
    slot_token = slot_token.at[flat_expert, slot_index].set(jnp.arange(TOKENS * TOP, dtype=jnp.int32) // TOP)

    def layer(tokens_in, gain_one, w_qkv, w_output, table_in, gain_two, w_router, w_first_all, w_second_all):
        normal_one = low(normed(tokens_in, gain_one))
        grouped = w_qkv.reshape(D, N_SHARD, 3, D // N_SHARD)
        w_query = grouped[:, :, 0, :].reshape(D, D)
        w_key = grouped[:, :, 1, :].reshape(D, D)
        w_value = grouped[:, :, 2, :].reshape(D, D)

        def one_sequence(pair):
            return attend(pair[0], pair[1], w_query, w_key, w_value, w_output, table_in)
        attn = lax.map(jax.checkpoint(one_sequence), (normal_one.reshape(N_EXPERT, TOK_DEV, D), lengths))
        state = tokens_in + attn.reshape(TOKENS, D)
        normal_two = low(normed(state, gain_two))
        logits = low_back(jnp.dot(normal_two, w_router, precision=HIGH))
        gates = gates_of(logits, routes)
        padded = jnp.concatenate([normal_two, jnp.zeros((1, D), jnp.float32)], axis=0)

        def expert_run(triple):
            w_first, w_second, picks = triple
            inputs = padded[picks]
            pre_act = low_back(jnp.dot(inputs, w_first, precision=HIGH))
            hidden_act = low(jax.nn.gelu(pre_act, approximate=True))
            return low_back(low(jnp.dot(hidden_act, w_second, precision=HIGH)))
        expert_rows = lax.map(jax.checkpoint(expert_run), (w_first_all, w_second_all, slot_token))
        chosen = expert_rows[flat_expert, slot_index].reshape(TOKENS, TOP, D)
        mixture = lax.optimization_barrier(jnp.sum(gates[:, :, None] * chosen, axis=1)) * valid[:, None]
        return state + mixture
    floats = (tokens.astype(jnp.float32), norm_gain1.astype(jnp.float32), qkv_weight.astype(jnp.float32), out_weight.astype(jnp.float32), rel_bias.astype(jnp.float32), norm_gain2.astype(jnp.float32), router_weight.astype(jnp.float32), in_weight.astype(jnp.float32), expert_out.astype(jnp.float32))
    result, pullback = jax.vjp(layer, *floats)
    grads = pullback(cotangent.astype(jnp.float32))
    return (result.astype(jnp.bfloat16), grads[0], grads[1], grads[2], grads[3], grads[4], grads[5], grads[6], grads[7], grads[8])
```

```python
import functools

import jax
import jax.numpy as jnp
import numpy as np
from jax import lax
from jax.experimental import pallas as pl
from jax.experimental.pallas import tpu as pltpu
from jax.sharding import PartitionSpec as P

HD = 64
TOP = 2
BUCKETS = 32
MAX_DIST = 128


EPSILON = 1e-06
MESH = pl.DeviceIdType.MESH
VMEM_LIMIT = 40 * 1024 * 1024
BF = jnp.bfloat16
F32 = jnp.float32


def remote(src, dst, send_sem, recv_sem, **where):
    return pltpu.make_async_remote_copy(
        src_ref=src,
        dst_ref=dst,
        send_sem=send_sem,
        recv_sem=recv_sem,
        device_id=where,
        device_id_type=MESH,
    )


def shard_peers():
    me = lax.axis_index("shard")
    near = me + 1 - 2 * lax.rem(me, 2)
    far = lax.rem(me + 2, 4)
    cross = lax.rem(near + 2, 4)
    return me, near, far, cross


def greet_shard(extra=0):
    barrier = pltpu.get_barrier_semaphore()
    _, near, far, _ = shard_peers()
    pl.semaphore_signal(barrier, inc=1, device_id={"shard": near}, device_id_type=MESH)
    pl.semaphore_signal(barrier, inc=1, device_id={"shard": far}, device_id_type=MESH)
    pl.semaphore_wait(barrier, 2 + extra)


def greet_expert(groups):
    barrier = pltpu.get_barrier_semaphore()
    here = lax.axis_index("expert")

    def greet(step, carry):
        pl.semaphore_signal(
            barrier, inc=1, device_id={"expert": lax.rem(here + step, groups)}, device_id_type=MESH
        )
        return carry

    lax.fori_loop(1, groups, greet, 0)


def loop(start, stop, body):
    def run(step, carry):
        body(step)
        return carry

    lax.fori_loop(start, stop, run, 0)


def call_kernel(body, ins, outs, scratch, collective):
    return pl.pallas_call(
        body,
        out_shape=outs,
        in_specs=[pl.BlockSpec(memory_space=pltpu.VMEM)] * len(ins),
        out_specs=[pl.BlockSpec(memory_space=pltpu.VMEM)] * len(outs),
        scratch_shapes=scratch,
        compiler_params=pltpu.CompilerParams(
            collective_id=collective, has_side_effects=True, vmem_limit_bytes=VMEM_LIMIT
        ),
    )(*ins)


def gather_kernel(count, *refs):
    ins, outs = refs[:count], refs[count : 2 * count]
    send, recv = refs[2 * count :]
    me, near, far, cross = shard_peers()
    greet_shard()
    first, second = [], []
    for i in range(count):
        one = remote(ins[i], outs[i].at[me], send.at[i, 0], recv.at[i, 0], shard=far)
        two = remote(ins[i], outs[i].at[me], send.at[i, 1], recv.at[i, 1], shard=near)
        one.start()
        two.start()
        first.append(one)
        second.append(two)
    for i in range(count):
        outs[i][me] = ins[i][...]
    for i in range(count):
        first[i].wait_recv()
        passed = remote(
            outs[i].at[far], outs[i].at[far], send.at[i, 2], recv.at[i, 2], shard=near
        )
        passed.start()
        second.append(passed)
    for i in range(count):
        first[i].wait_send()
    for copy in second:
        copy.wait()


def shard_gather(arrays, collective):
    count = len(arrays)
    return call_kernel(
        functools.partial(gather_kernel, count),
        arrays,
        [jax.ShapeDtypeStruct((4,) + a.shape, a.dtype) for a in arrays],
        [pltpu.SemaphoreType.DMA((count, 3)), pltpu.SemaphoreType.DMA((count, 3))],
        collective,
    )


def sum_kernel(x, out, got, mid, last, send, recv):
    me, near, far, cross = shard_peers()
    greet_shard()
    one = remote(x.at[cross], got.at[1], send.at[0], recv.at[0], shard=near)
    two = remote(x.at[near], got.at[0], send.at[1], recv.at[1], shard=near)
    one.start()
    two.start()
    one.wait_recv()
    mid[...] = (x[far].astype(F32) + got[1].astype(F32)).astype(BF)
    three = remote(mid, last, send.at[2], recv.at[2], shard=far)
    three.start()
    two.wait_recv()
    three.wait_recv()
    out[me] = (x[me].astype(F32) + got[0].astype(F32) + last[...].astype(F32)).astype(BF)
    four = remote(out.at[me], out.at[me], send.at[3], recv.at[3], shard=far)
    five = remote(out.at[me], out.at[me], send.at[4], recv.at[4], shard=near)
    four.start()
    five.start()
    four.wait_recv()
    six = remote(out.at[far], out.at[far], send.at[5], recv.at[5], shard=near)
    six.start()
    five.wait_recv()
    six.wait_recv()
    for copy in (one, two, three, four, five, six):
        copy.wait_send()


def shard_sum(blocks, collective):
    _, rows, columns = blocks.shape
    return call_kernel(
        sum_kernel,
        [blocks],
        [jax.ShapeDtypeStruct(blocks.shape, BF)],
        [
            pltpu.VMEM((2, rows, columns), BF),
            pltpu.VMEM((rows, columns), BF),
            pltpu.VMEM((rows, columns), BF),
            pltpu.SemaphoreType.DMA((6,)),
            pltpu.SemaphoreType.DMA((6,)),
        ],
        collective,
    )[0]


def dispatch_kernel(groups, x, out, s0, r0, s1, r1, s2, r2, s3, r3):
    here = lax.axis_index("expert")
    me, near, far, cross = shard_peers()
    greet_expert(groups)
    greet_shard(groups - 1)

    def origin(step):
        return lax.rem(here + groups - step, groups)

    def sent(step):
        there = lax.rem(here + step, groups)
        return remote(x.at[there], out.at[me, here], s0.at[step], r0.at[step], expert=there)

    def block(step, place, send, recv, peer):
        at = origin(step)
        return remote(
            out.at[place, at], out.at[place, at], send.at[step], recv.at[step], shard=peer
        )

    def spread(step):
        block(step, me, s2, r2, far).start()
        block(step, me, s1, r1, near).start()

    def passed(step):
        block(step, far, s2, r2, far).wait_recv()
        block(step, far, s3, r3, near).start()

    loop(1, groups, lambda step: sent(step).start())
    out[me, here] = x[here]
    spread(0)

    def middle(step):
        at = origin(step)
        remote(x.at[at], out.at[me, at], s0.at[step], r0.at[step], expert=at).wait_recv()
        spread(step)
        passed(step - 1)

    loop(1, groups, middle)
    passed(groups - 1)

    def finish(step):
        block(step, near, s1, r1, near).wait_recv()
        block(step, cross, s3, r3, near).wait_recv()
        block(step, me, s1, r1, near).wait_send()
        block(step, me, s2, r2, far).wait_send()
        block(step, far, s3, r3, near).wait_send()

    loop(0, groups, finish)
    loop(1, groups, lambda step: sent(step).wait_send())


def dispatch(blocks, collective):
    groups = blocks.shape[0]
    return call_kernel(
        functools.partial(dispatch_kernel, groups),
        [blocks],
        [jax.ShapeDtypeStruct((4,) + blocks.shape, BF)],
        [pltpu.SemaphoreType.DMA((groups,))] * 8,
        collective,
    )[0]


def combine_kernel(groups, x, out, got, mid, last, done, s0, r0, s1, r1, s2, r2, s3, r3):
    here = lax.axis_index("expert")
    me, near, far, cross = shard_peers()
    greet_expert(groups)
    greet_shard(groups - 1)

    def place(step):
        return lax.rem(here + 1 + step, groups)

    def first(step):
        at = place(step)
        return remote(x.at[cross, at], got.at[1, at], s0.at[step], r0.at[step], shard=near)

    def second(step):
        at = place(step)
        return remote(x.at[near, at], got.at[0, at], s1.at[step], r1.at[step], shard=near)

    def third(step):
        at = place(step)
        return remote(mid.at[at], last.at[at], s2.at[step], r2.at[step], shard=far)

    def home(step):
        at = place(step)
        return remote(done.at[at], out.at[here], s3.at[step], r3.at[step], expert=at)

    def begin(step):
        first(step).start()
        second(step).start()

    def half(step):
        at = place(step)
        first(step).wait_recv()
        mid[at] = (x[far, at].astype(F32) + got[1, at].astype(F32)).astype(BF)
        third(step).start()

    def whole(step):
        at = place(step)
        second(step).wait_recv()
        third(step).wait_recv()
        return (
            x[me, at].astype(F32) + got[0, at].astype(F32) + last[at].astype(F32)
        ).astype(BF)

    def back(step):
        done[place(step)] = whole(step)
        home(step).start()

    loop(0, groups, begin)
    half(0)

    def middle(step):
        half(step)
        back(step - 1)

    loop(1, groups, middle)
    out[here] = whole(groups - 1)

    def finish(step):
        source = lax.rem(here + groups - 1 - step, groups)
        remote(
            done.at[source], out.at[source], s3.at[step], r3.at[step], expert=source
        ).wait_recv()
        home(step).wait_send()

    loop(0, groups - 1, finish)

    def sent(step):
        first(step).wait_send()
        second(step).wait_send()
        third(step).wait_send()

    loop(0, groups, sent)


def combine(blocks, collective):
    groups = blocks.shape[1]
    shape = blocks.shape[1:]
    return call_kernel(
        functools.partial(combine_kernel, groups),
        [blocks],
        [jax.ShapeDtypeStruct(shape, BF)],
        [
            pltpu.VMEM((2,) + shape, BF),
            pltpu.VMEM(shape, BF),
            pltpu.VMEM(shape, BF),
            pltpu.VMEM(shape, BF),
        ]
        + [pltpu.SemaphoreType.DMA((groups,))] * 8,
        collective,
    )[0]


def total_kernel(count, lines, *refs):
    ins, outs = refs[:count], refs[count : 2 * count]
    got, mid, parts = (refs[(2 + i) * count : (3 + i) * count] for i in range(3))
    sa, ra, sb, rb, sc, rc, sd, rd = refs[5 * count :]
    here = lax.axis_index("expert")
    side = lax.rem(here, 2)
    line = here // 2
    partner = here + 1 - 2 * side
    other = 1 - side
    barrier = pltpu.get_barrier_semaphore()
    pl.semaphore_signal(barrier, inc=1, device_id={"expert": partner}, device_id_type=MESH)

    def on_line(step):
        return lax.rem(line + step, lines)

    def from_line(step):
        return lax.rem(line + lines - step, lines)

    def greet(step):
        pl.semaphore_signal(
            barrier, inc=1, device_id={"expert": 2 * on_line(step) + side}, device_id_type=MESH
        )

    loop(1, lines, greet)
    pl.semaphore_wait(barrier, lines)

    def cross(i, step):
        at = on_line(step)
        return remote(
            ins[i].at[other, at], got[i].at[at], sa.at[i, step], ra.at[i, step], expert=partner
        )

    def along(i, step, at):
        return remote(
            mid[i].at[at], parts[i].at[line], sb.at[i, step], rb.at[i, step],
            expert=2 * at + side,
        )

    def arrive(i, step):
        at = from_line(step)
        return remote(
            mid[i].at[at], parts[i].at[at], sb.at[i, step], rb.at[i, step], expert=2 * at + side
        )

    def result(i, step):
        at = on_line(step)
        return remote(
            outs[i].at[side, line], outs[i].at[side, line], sc.at[i, step], rc.at[i, step],
            expert=2 * at + side,
        )

    def landed(i, step):
        at = from_line(step)
        return remote(
            outs[i].at[side, at], outs[i].at[side, at], sc.at[i, step], rc.at[i, step],
            expert=2 * at + side,
        )

    def shared(i, step, where):
        at = from_line(step)
        return remote(
            outs[i].at[where, at], outs[i].at[where, at], sd.at[i, step], rd.at[i, step],
            expert=partner,
        )

    def crossing(step):
        for i in range(count):
            cross(i, step).start()

    loop(1, lines, crossing)
    crossing(0)

    def paired(step):
        at = on_line(step)
        for i in range(count):
            cross(i, step).wait_recv()
            mid[i][at] = (ins[i][side, at].astype(F32) + got[i][at].astype(F32)).astype(
                ins[i].dtype
            )
            along(i, step, at).start()

    loop(1, lines, paired)
    for i in range(count):
        cross(i, 0).wait_recv()
        parts[i][line] = (ins[i][side, line].astype(F32) + got[i][line].astype(F32)).astype(
            ins[i].dtype
        )

    def arrived(step):
        for i in range(count):
            arrive(i, step).wait_recv()

    loop(1, lines, arrived)
    for i in range(count):
        added = parts[i][0].astype(F32)
        for at in range(1, lines):
            added = added + parts[i][at].astype(F32)
        outs[i][side, line] = added.astype(ins[i].dtype)

    def publish(step):
        for i in range(count):
            result(i, step).start()

    loop(1, lines, publish)
    for i in range(count):
        shared(i, 0, side).start()

    def relay(step):
        for i in range(count):
            landed(i, step).wait_recv()
            shared(i, step, side).start()

    loop(1, lines, relay)

    def finish(step):
        for i in range(count):
            shared(i, step, other).wait_recv()
            shared(i, step, side).wait_send()
            cross(i, step).wait_send()

    loop(0, lines, finish)

    def sent(step):
        for i in range(count):
            along(i, step, on_line(step)).wait_send()
            result(i, step).wait_send()

    loop(1, lines, sent)


def expert_sum(arrays, collective):
    count, lines = len(arrays), arrays[0].shape[1]
    room = [pltpu.VMEM(a.shape[1:], a.dtype) for a in arrays]
    return call_kernel(
        functools.partial(total_kernel, count, lines),
        arrays,
        [jax.ShapeDtypeStruct(a.shape, a.dtype) for a in arrays],
        room * 3 + [pltpu.SemaphoreType.DMA((count, lines))] * 8,
        collective,
    )


def bucket_of(distance):
    half = BUCKETS // 2
    powers = np.arange(1, half)
    edges = np.ceil(half * (MAX_DIST / half) ** (powers / half))
    counted = jnp.zeros(distance.shape, jnp.int32)
    for threshold in edges:
        counted = counted + (distance >= int(threshold)).astype(jnp.int32)
    return jnp.where(distance < half, distance, half + counted)


def normed(values, gain):
    return values * lax.rsqrt(jnp.mean(values * values, axis=-1, keepdims=True) + EPSILON) * gain


def gates_of(logits, routes):
    probability = jax.nn.softmax(logits, axis=-1)
    chosen = routes[:, :, None] == jnp.arange(logits.shape[1])[None, None, :]
    picked = jnp.sum(jnp.where(chosen, probability[:, None, :], 0.0), axis=2)
    return picked / jnp.sum(picked, axis=1, keepdims=True)


def bias_matrix(table, span):
    heads_here = table.shape[0]
    distance = jnp.arange(span, dtype=jnp.int32)
    table_hot = (bucket_of(distance)[:, None] == jnp.arange(table.shape[1])[None, :]).astype(
        jnp.float32
    )
    by_distance = jnp.dot(table, table_hot.T, precision=lax.Precision.HIGHEST)
    reversed_pad = jnp.concatenate(
        [by_distance[:, ::-1], jnp.zeros((heads_here, span), jnp.float32)], axis=1
    )
    tiled = jnp.tile(reversed_pad, (1, span))[:, : span * (2 * span - 1)]
    return tiled.reshape(heads_here, span, 2 * span - 1)[:, :, span - 1 :]


def scores_of(queries, keys_low, bias_mat, allowed, scale):
    raw_scores = (
        jnp.einsum("ihd,jhd->hij", queries, keys_low, preferred_element_type=jnp.float32) * scale
        + bias_mat
    )
    return jnp.where(allowed[None], raw_scores, -1000000000.0)


def contract_first(left, right):
    return lax.dot_general(
        left, right, (((0,), (0,)), ((), ())), preferred_element_type=jnp.float32
    )


def contract_last(left, right):
    return lax.dot_general(
        left, right, (((1,), (1,)), ((), ())), preferred_element_type=jnp.float32
    )


def wide(blocks):
    return blocks.transpose(1, 0, 2).reshape(blocks.shape[1], -1)


def narrow(full, share):
    return full.reshape(full.shape[0], -1, share).transpose(1, 0, 2)


def per_device(
    tokens,
    norm_gain1,
    qkv_weight,
    out_weight,
    rel_bias,
    norm_gain2,
    router_weight,
    in_weight,
    expert_out,
    lengths,
    routes,
    cotangent,
):
    span = tokens.shape[0]
    share = tokens.shape[1]
    width = qkv_weight.shape[0]
    heads_here = rel_bias.shape[0]
    groups = lax.axis_size("expert")
    shard_count = lax.axis_size("shard")
    experts_all = router_weight.shape[1]
    capacity = -(-(3 * span * TOP // (2 * experts_all)) // 16) * 16
    slots_all = experts_all * capacity
    shard_at = lax.axis_index("shard")
    scale = HD ** (-0.5)
    positions = jnp.arange(span, dtype=jnp.int32)
    valid = (positions < lengths[0]).astype(jnp.float32)
    allowed = (positions[None, :] <= positions[:, None]) & (positions[None, :] < lengths[0])
    token_blocks, grad_blocks = shard_gather([tokens, cotangent], 1)
    tokens_full = wide(token_blocks).astype(jnp.float32)
    normal_one = normed(tokens_full, norm_gain1).astype(jnp.bfloat16)
    projected = jnp.dot(normal_one, qkv_weight, preferred_element_type=jnp.float32).astype(
        jnp.bfloat16
    )
    queries = projected[:, :share].reshape(span, heads_here, HD)
    keys_low = projected[:, share : 2 * share].reshape(span, heads_here, HD)
    values_low = projected[:, 2 * share :].reshape(span, heads_here, HD)
    bias_mat = bias_matrix(rel_bias, span)
    scores = scores_of(queries, keys_low, bias_mat, allowed, scale)
    log_total = jax.nn.logsumexp(scores, axis=-1, keepdims=True)
    probability = jnp.exp(scores - log_total)
    weights_low = probability.astype(jnp.bfloat16)
    attended = jnp.einsum(
        "hij,jhd->ihd", weights_low, values_low, preferred_element_type=jnp.float32
    )
    attended = attended.reshape(span, share).astype(jnp.bfloat16)
    attn_term = jnp.dot(attended, out_weight, preferred_element_type=jnp.float32) * valid[:, None]
    attn_blocks = shard_sum(narrow(attn_term.astype(jnp.bfloat16), share), 2)
    state_blocks = token_blocks.astype(jnp.float32) + attn_blocks.astype(jnp.float32)
    state_own = lax.dynamic_index_in_dim(state_blocks, shard_at, 0, keepdims=False)
    state_full = wide(state_blocks)
    normal_two = normed(state_full, norm_gain2).astype(jnp.bfloat16)
    normal_two_own = lax.dynamic_slice_in_dim(normal_two, shard_at * share, share, 1)
    logits = jnp.dot(normal_two, router_weight, preferred_element_type=jnp.float32)
    gates = gates_of(logits, routes)
    named = (
        routes[:, :, None] == jnp.arange(experts_all, dtype=jnp.int32)[None, None, :]
    ).astype(jnp.float32)
    earlier = (positions[None, :] < positions[:, None]).astype(jnp.bfloat16)
    before = jnp.dot(
        earlier,
        jnp.sum(named, axis=1).astype(jnp.bfloat16),
        preferred_element_type=jnp.float32,
    )
    ranks = jnp.sum(named * before[:, None, :], axis=2).astype(jnp.int32)
    slot_index = routes * capacity + ranks
    by_choice = jnp.concatenate([slot_index[:, 0], slot_index[:, 1]], axis=0)
    placing = (by_choice[:, None] == jnp.arange(slots_all, dtype=jnp.int32)[None, :]).astype(
        jnp.bfloat16
    )
    grad_own = cotangent.astype(jnp.float32)
    weighted = gates * valid[:, None]
    sources = jnp.concatenate(
        [
            jnp.concatenate([normal_two_own, normal_two_own], axis=0),
            jnp.concatenate(
                [
                    (weighted[:, 0:1] * grad_own).astype(jnp.bfloat16),
                    (weighted[:, 1:2] * grad_own).astype(jnp.bfloat16),
                ],
                axis=0,
            ),
        ],
        axis=1,
    )
    placed_rows = contract_first(placing, sources).astype(jnp.bfloat16)
    outgoing = placed_rows.reshape(groups, capacity, 2, share).transpose(0, 2, 1, 3)
    incoming = dispatch(outgoing, 3)
    incoming = incoming.transpose(2, 1, 3, 0, 4).reshape(2, slots_all, width)
    arrived, grad_arrived = incoming[0], incoming[1]
    pre_act = jnp.dot(arrived, in_weight[0], preferred_element_type=jnp.float32)
    gelu_value, gelu_back = jax.vjp(lambda inner: jax.nn.gelu(inner, approximate=True), pre_act)
    hidden_act = gelu_value.astype(jnp.bfloat16)
    partial_out = jnp.dot(hidden_act, expert_out[0], preferred_element_type=jnp.float32)
    hidden_grad = contract_last(grad_arrived, expert_out[0])
    pre_grad = gelu_back(hidden_grad)[0].astype(jnp.bfloat16)
    input_grad = contract_last(pre_grad, in_weight[0])
    partials = jnp.stack(
        [partial_out.astype(jnp.bfloat16), input_grad.astype(jnp.bfloat16)], axis=0
    )
    partials = partials.reshape(2, groups, capacity, shard_count, share).transpose(3, 1, 0, 2, 4)
    returned = combine(partials, 4)
    grad_expert_out = contract_first(hidden_act, grad_arrived)[None]
    grad_in_weight = contract_first(arrived, pre_grad)[None]
    returned = returned.transpose(0, 2, 1, 3).reshape(slots_all, 2 * share)
    picked = jnp.dot(placing, returned, preferred_element_type=jnp.float32)
    picked = picked.reshape(TOP, span, 2, share)
    picked_out = picked[:, :, 0].transpose(1, 0, 2)
    mixture = jnp.sum(gates[:, :, None] * picked_out, axis=1) * valid[:, None]
    output = (state_own + mixture).astype(jnp.bfloat16)
    gate_part = jnp.sum(grad_own[:, None, :] * picked_out, axis=2) * valid[:, None]
    normal_two_share = picked[0, :, 1] + picked[1, :, 1]
    gate_rows = jnp.concatenate([gate_part.T, jnp.zeros((8 - TOP, span), jnp.float32)], axis=0)
    normal_two_blocks, gate_blocks = shard_gather(
        [normal_two_share.astype(jnp.bfloat16), gate_rows], 5
    )
    normal_two_grad = wide(normal_two_blocks).astype(jnp.float32)
    gate_grad = jnp.sum(gate_blocks, axis=0)[:TOP].T
    grad_full = wide(grad_blocks).astype(jnp.float32)
    gate_value, gate_back = jax.vjp(lambda inner: gates_of(inner, routes), logits)
    logit_grad = gate_back(gate_grad)[0].astype(jnp.bfloat16)
    grad_router = contract_first(normal_two, logit_grad)
    normal_two_grad = normal_two_grad + contract_last(logit_grad, router_weight)
    norm_value, norm_two_back = jax.vjp(normed, state_full, norm_gain2)
    state_grad_part, grad_gain2 = norm_two_back(normal_two_grad)
    state_grad = grad_full + state_grad_part
    attn_grad = (state_grad * valid[:, None]).astype(jnp.bfloat16)
    grad_out_weight = contract_first(attended, attn_grad)
    attended_grad = (
        contract_last(attn_grad, out_weight).astype(jnp.bfloat16).reshape(span, heads_here, HD)
    )
    value_grad = jnp.einsum(
        "hij,ihd->jhd", weights_low, attended_grad, preferred_element_type=jnp.float32
    )
    prob_grad = jnp.einsum(
        "ihd,jhd->hij", attended_grad, values_low, preferred_element_type=jnp.float32
    )
    score_grad = (
        probability * (prob_grad - jnp.sum(probability * prob_grad, axis=-1, keepdims=True))
    ).astype(jnp.bfloat16)
    query_grad = (
        jnp.einsum("hij,jhd->ihd", score_grad, keys_low, preferred_element_type=jnp.float32) * scale
    )
    key_grad = (
        jnp.einsum("hij,ihd->jhd", score_grad, queries, preferred_element_type=jnp.float32) * scale
    )
    bias_value, bias_back = jax.vjp(lambda table: bias_matrix(table, span), rel_bias)
    grad_rel_bias = bias_back(score_grad.astype(jnp.float32))[0]
    projected_grad = jnp.concatenate(
        [
            query_grad.reshape(span, share),
            key_grad.reshape(span, share),
            value_grad.reshape(span, share),
        ],
        axis=1,
    ).astype(jnp.bfloat16)
    grad_qkv = contract_first(normal_one, projected_grad)
    normal_one_part = contract_last(projected_grad, qkv_weight)
    normal_one_blocks = shard_sum(narrow(normal_one_part.astype(jnp.bfloat16), share), 6)
    normal_one_grad = wide(normal_one_blocks).astype(jnp.float32)
    first_value, norm_one_back = jax.vjp(normed, tokens_full, norm_gain1)
    token_grad_part, grad_gain1 = norm_one_back(normal_one_grad)
    token_grad = lax.dynamic_slice_in_dim(state_grad + token_grad_part, shard_at * share, share, 1)
    columns = 3 * share
    dense = jnp.concatenate(
        [
            grad_qkv.astype(jnp.bfloat16),
            grad_out_weight.astype(jnp.bfloat16).reshape(-1, columns),
        ],
        axis=0,
    )
    rows = dense.shape[0] // groups
    small_parts = [grad_rel_bias, grad_gain1, grad_gain2, grad_router]
    small = jnp.concatenate([part.reshape(-1) for part in small_parts])
    small_rows = -(-small.shape[0] // (groups * 1024)) * 8
    small = jnp.pad(small, (0, groups * small_rows * 128 - small.shape[0]))
    dense, small = expert_sum(
        [
            dense.reshape(2, groups // 2, rows, columns),
            small.reshape(2, groups // 2, small_rows, 128),
        ],
        7,
    )
    dense = dense.reshape(groups * rows, columns).astype(jnp.float32)
    small = small.reshape(-1)
    summed, start = [], 0
    for part in small_parts:
        summed.append(small[start : start + part.size].reshape(part.shape))
        start += part.size
    return (
        output,
        token_grad,
        summed[1],
        dense[:width],
        dense[width:].reshape(grad_out_weight.shape),
        summed[0],
        summed[2],
        summed[3],
        grad_in_weight,
        grad_expert_out,
    )


def solution(mesh):
    placed = (
        P("expert", "shard"),
        P(),
        P(None, "shard"),
        P("shard", None),
        P("shard", None),
        P(),
        P(),
        P("expert", None, "shard"),
        P("expert", "shard", None),
        P("expert"),
        P("expert", None),
        P("expert", "shard"),
    )
    return jax.shard_map(
        per_device,
        mesh=mesh,
        in_specs=placed,
        out_specs=(
            P("expert", "shard"),
            P("expert", "shard"),
            P(),
            P(None, "shard"),
            P("shard", None),
            P("shard", None),
            P(),
            P(),
            P("expert", None, "shard"),
            P("expert", "shard", None),
        ),
        check_vma=False,
    )
```

```python
import functools

import jax
import jax.numpy as jnp
import numpy as np
from jax import lax
from jax.experimental import pallas as pl
from jax.experimental.pallas import tpu as pltpu
from jax.sharding import PartitionSpec as P

HD = 64
TOP = 2
BUCKETS = 32
MAX_DIST = 128


EPSILON = 1e-06
MESH = pl.DeviceIdType.MESH
VMEM_LIMIT = 40 * 1024 * 1024
BF = jnp.bfloat16
F32 = jnp.float32


def remote(src, dst, send_sem, recv_sem, **where):
    return pltpu.make_async_remote_copy(
        src_ref=src,
        dst_ref=dst,
        send_sem=send_sem,
        recv_sem=recv_sem,
        device_id=where,
        device_id_type=MESH,
    )


def shard_peers():
    me = lax.axis_index("shard")
    near = me + 1 - 2 * lax.rem(me, 2)
    far = lax.rem(me + 2, 4)
    cross = lax.rem(near + 2, 4)
    return me, near, far, cross


def greet_shard(extra=0):
    barrier = pltpu.get_barrier_semaphore()
    _, near, far, _ = shard_peers()
    pl.semaphore_signal(barrier, inc=1, device_id={"shard": near}, device_id_type=MESH)
    pl.semaphore_signal(barrier, inc=1, device_id={"shard": far}, device_id_type=MESH)
    pl.semaphore_wait(barrier, 2 + extra)


def greet_expert(groups):
    barrier = pltpu.get_barrier_semaphore()
    here = lax.axis_index("expert")

    def greet(step, carry):
        pl.semaphore_signal(
            barrier, inc=1, device_id={"expert": lax.rem(here + step, groups)}, device_id_type=MESH
        )
        return carry

    lax.fori_loop(1, groups, greet, 0)


def loop(start, stop, body):
    def run(step, carry):
        body(step)
        return carry

    lax.fori_loop(start, stop, run, 0)


def call_kernel(body, ins, outs, scratch, collective):
    return pl.pallas_call(
        body,
        out_shape=outs,
        in_specs=[pl.BlockSpec(memory_space=pltpu.VMEM)] * len(ins),
        out_specs=[pl.BlockSpec(memory_space=pltpu.VMEM)] * len(outs),
        scratch_shapes=scratch,
        compiler_params=pltpu.CompilerParams(
            collective_id=collective, has_side_effects=True, vmem_limit_bytes=VMEM_LIMIT
        ),
    )(*ins)


def gather_kernel(count, *refs):
    ins, outs = refs[:count], refs[count : 2 * count]
    send, recv = refs[2 * count :]
    me, near, far, cross = shard_peers()
    greet_shard()
    first, second = [], []
    for i in range(count):
        one = remote(ins[i], outs[i].at[me], send.at[i, 0], recv.at[i, 0], shard=far)
        two = remote(ins[i], outs[i].at[me], send.at[i, 1], recv.at[i, 1], shard=near)
        one.start()
        two.start()
        first.append(one)
        second.append(two)
    for i in range(count):
        outs[i][me] = ins[i][...]
    for i in range(count):
        first[i].wait_recv()
        passed = remote(
            outs[i].at[far], outs[i].at[far], send.at[i, 2], recv.at[i, 2], shard=near
        )
        passed.start()
        second.append(passed)
    for i in range(count):
        first[i].wait_send()
    for copy in second:
        copy.wait()


def shard_gather(arrays, collective):
    count = len(arrays)
    return call_kernel(
        functools.partial(gather_kernel, count),
        arrays,
        [jax.ShapeDtypeStruct((4,) + a.shape, a.dtype) for a in arrays],
        [pltpu.SemaphoreType.DMA((count, 3)), pltpu.SemaphoreType.DMA((count, 3))],
        collective,
    )


def sum_kernel(x, out, got, mid, last, send, recv):
    me, near, far, cross = shard_peers()
    greet_shard()
    one = remote(x.at[cross], got.at[1], send.at[0], recv.at[0], shard=near)
    two = remote(x.at[near], got.at[0], send.at[1], recv.at[1], shard=near)
    one.start()
    two.start()
    one.wait_recv()
    mid[...] = (x[far].astype(F32) + got[1].astype(F32)).astype(BF)
    three = remote(mid, last, send.at[2], recv.at[2], shard=far)
    three.start()
    two.wait_recv()
    three.wait_recv()
    out[me] = (x[me].astype(F32) + got[0].astype(F32) + last[...].astype(F32)).astype(BF)
    four = remote(out.at[me], out.at[me], send.at[3], recv.at[3], shard=far)
    five = remote(out.at[me], out.at[me], send.at[4], recv.at[4], shard=near)
    four.start()
    five.start()
    four.wait_recv()
    six = remote(out.at[far], out.at[far], send.at[5], recv.at[5], shard=near)
    six.start()
    five.wait_recv()
    six.wait_recv()
    for copy in (one, two, three, four, five, six):
        copy.wait_send()


def shard_sum(blocks, collective):
    _, rows, columns = blocks.shape
    return call_kernel(
        sum_kernel,
        [blocks],
        [jax.ShapeDtypeStruct(blocks.shape, BF)],
        [
            pltpu.VMEM((2, rows, columns), BF),
            pltpu.VMEM((rows, columns), BF),
            pltpu.VMEM((rows, columns), BF),
            pltpu.SemaphoreType.DMA((6,)),
            pltpu.SemaphoreType.DMA((6,)),
        ],
        collective,
    )[0]


def dispatch_kernel(groups, x, out, s0, r0, s1, r1, s2, r2, s3, r3):
    here = lax.axis_index("expert")
    me, near, far, cross = shard_peers()
    greet_expert(groups)
    greet_shard(groups - 1)

    def origin(step):
        return lax.rem(here + groups - step, groups)

    def sent(step):
        there = lax.rem(here + step, groups)
        return remote(x.at[there], out.at[me, here], s0.at[step], r0.at[step], expert=there)

    def block(step, place, send, recv, peer):
        at = origin(step)
        return remote(
            out.at[place, at], out.at[place, at], send.at[step], recv.at[step], shard=peer
        )

    def spread(step):
        block(step, me, s2, r2, far).start()
        block(step, me, s1, r1, near).start()

    def passed(step):
        block(step, far, s2, r2, far).wait_recv()
        block(step, far, s3, r3, near).start()

    loop(1, groups, lambda step: sent(step).start())
    out[me, here] = x[here]
    spread(0)

    def middle(step):
        at = origin(step)
        remote(x.at[at], out.at[me, at], s0.at[step], r0.at[step], expert=at).wait_recv()
        spread(step)
        passed(step - 1)

    loop(1, groups, middle)
    passed(groups - 1)

    def finish(step):
        block(step, near, s1, r1, near).wait_recv()
        block(step, cross, s3, r3, near).wait_recv()
        block(step, me, s1, r1, near).wait_send()
        block(step, me, s2, r2, far).wait_send()
        block(step, far, s3, r3, near).wait_send()

    loop(0, groups, finish)
    loop(1, groups, lambda step: sent(step).wait_send())


def dispatch(blocks, collective):
    groups = blocks.shape[0]
    return call_kernel(
        functools.partial(dispatch_kernel, groups),
        [blocks],
        [jax.ShapeDtypeStruct((4,) + blocks.shape, BF)],
        [pltpu.SemaphoreType.DMA((groups,))] * 8,
        collective,
    )[0]


def combine_kernel(groups, x, out, got, mid, last, done, s0, r0, s1, r1, s2, r2, s3, r3):
    here = lax.axis_index("expert")
    me, near, far, cross = shard_peers()
    greet_expert(groups)
    greet_shard(groups - 1)

    def place(step):
        return lax.rem(here + 1 + step, groups)

    def first(step):
        at = place(step)
        return remote(x.at[cross, at], got.at[1, at], s0.at[step], r0.at[step], shard=near)

    def second(step):
        at = place(step)
        return remote(x.at[near, at], got.at[0, at], s1.at[step], r1.at[step], shard=near)

    def third(step):
        at = place(step)
        return remote(mid.at[at], last.at[at], s2.at[step], r2.at[step], shard=far)

    def home(step):
        at = place(step)
        return remote(done.at[at], out.at[here], s3.at[step], r3.at[step], expert=at)

    def begin(step):
        first(step).start()
        second(step).start()

    def half(step):
        at = place(step)
        first(step).wait_recv()
        mid[at] = (x[far, at].astype(F32) + got[1, at].astype(F32)).astype(BF)
        third(step).start()

    def whole(step):
        at = place(step)
        second(step).wait_recv()
        third(step).wait_recv()
        return (
            x[me, at].astype(F32) + got[0, at].astype(F32) + last[at].astype(F32)
        ).astype(BF)

    def back(step):
        done[place(step)] = whole(step)
        home(step).start()

    loop(0, groups, begin)
    half(0)

    def middle(step):
        half(step)
        back(step - 1)

    loop(1, groups, middle)
    out[here] = whole(groups - 1)

    def finish(step):
        source = lax.rem(here + groups - 1 - step, groups)
        remote(
            done.at[source], out.at[source], s3.at[step], r3.at[step], expert=source
        ).wait_recv()
        home(step).wait_send()

    loop(0, groups - 1, finish)

    def sent(step):
        first(step).wait_send()
        second(step).wait_send()
        third(step).wait_send()

    loop(0, groups, sent)


def combine(blocks, collective):
    groups = blocks.shape[1]
    shape = blocks.shape[1:]
    return call_kernel(
        functools.partial(combine_kernel, groups),
        [blocks],
        [jax.ShapeDtypeStruct(shape, BF)],
        [
            pltpu.VMEM((2,) + shape, BF),
            pltpu.VMEM(shape, BF),
            pltpu.VMEM(shape, BF),
            pltpu.VMEM(shape, BF),
        ]
        + [pltpu.SemaphoreType.DMA((groups,))] * 8,
        collective,
    )[0]


def total_kernel(count, lines, *refs):
    ins, outs = refs[:count], refs[count : 2 * count]
    got, mid, parts = (refs[(2 + i) * count : (3 + i) * count] for i in range(3))
    sa, ra, sb, rb, sc, rc, sd, rd = refs[5 * count :]
    here = lax.axis_index("expert")
    side = lax.rem(here, 2)
    line = here // 2
    partner = here + 1 - 2 * side
    other = 1 - side
    barrier = pltpu.get_barrier_semaphore()
    pl.semaphore_signal(barrier, inc=1, device_id={"expert": partner}, device_id_type=MESH)

    def on_line(step):
        return lax.rem(line + step, lines)

    def from_line(step):
        return lax.rem(line + lines - step, lines)

    def greet(step):
        pl.semaphore_signal(
            barrier, inc=1, device_id={"expert": 2 * on_line(step) + side}, device_id_type=MESH
        )

    loop(1, lines, greet)
    pl.semaphore_wait(barrier, lines)

    def cross(i, step):
        at = on_line(step)
        return remote(
            ins[i].at[other, at], got[i].at[at], sa.at[i, step], ra.at[i, step], expert=partner
        )

    def along(i, step, at):
        return remote(
            mid[i].at[at], parts[i].at[line], sb.at[i, step], rb.at[i, step],
            expert=2 * at + side,
        )

    def arrive(i, step):
        at = from_line(step)
        return remote(
            mid[i].at[at], parts[i].at[at], sb.at[i, step], rb.at[i, step], expert=2 * at + side
        )

    def result(i, step):
        at = on_line(step)
        return remote(
            outs[i].at[side, line], outs[i].at[side, line], sc.at[i, step], rc.at[i, step],
            expert=2 * at + side,
        )

    def landed(i, step):
        at = from_line(step)
        return remote(
            outs[i].at[side, at], outs[i].at[side, at], sc.at[i, step], rc.at[i, step],
            expert=2 * at + side,
        )

    def shared(i, step, where):
        at = from_line(step)
        return remote(
            outs[i].at[where, at], outs[i].at[where, at], sd.at[i, step], rd.at[i, step],
            expert=partner,
        )

    def crossing(step):
        for i in range(count):
            cross(i, step).start()

    loop(1, lines, crossing)
    crossing(0)

    def paired(step):
        at = on_line(step)
        for i in range(count):
            cross(i, step).wait_recv()
            mid[i][at] = (ins[i][side, at].astype(F32) + got[i][at].astype(F32)).astype(
                ins[i].dtype
            )
            along(i, step, at).start()

    loop(1, lines, paired)
    for i in range(count):
        cross(i, 0).wait_recv()
        parts[i][line] = (ins[i][side, line].astype(F32) + got[i][line].astype(F32)).astype(
            ins[i].dtype
        )

    def arrived(step):
        for i in range(count):
            arrive(i, step).wait_recv()

    loop(1, lines, arrived)
    for i in range(count):
        added = parts[i][0].astype(F32)
        for at in range(1, lines):
            added = added + parts[i][at].astype(F32)
        outs[i][side, line] = added.astype(ins[i].dtype)

    def publish(step):
        for i in range(count):
            result(i, step).start()

    loop(1, lines, publish)
    for i in range(count):
        shared(i, 0, side).start()

    def relay(step):
        for i in range(count):
            landed(i, step).wait_recv()
            shared(i, step, side).start()

    loop(1, lines, relay)

    def finish(step):
        for i in range(count):
            shared(i, step, other).wait_recv()
            shared(i, step, side).wait_send()
            cross(i, step).wait_send()

    loop(0, lines, finish)

    def sent(step):
        for i in range(count):
            along(i, step, on_line(step)).wait_send()
            result(i, step).wait_send()

    loop(1, lines, sent)


def expert_sum(arrays, collective):
    count, lines = len(arrays), arrays[0].shape[1]
    room = [pltpu.VMEM(a.shape[1:], a.dtype) for a in arrays]
    return call_kernel(
        functools.partial(total_kernel, count, lines),
        arrays,
        [jax.ShapeDtypeStruct(a.shape, a.dtype) for a in arrays],
        room * 3 + [pltpu.SemaphoreType.DMA((count, lines))] * 8,
        collective,
    )


def bucket_of(distance):
    half = BUCKETS // 2
    powers = np.arange(1, half)
    edges = np.ceil(half * (MAX_DIST / half) ** (powers / half))
    counted = jnp.zeros(distance.shape, jnp.int32)
    for threshold in edges:
        counted = counted + (distance >= int(threshold)).astype(jnp.int32)
    return jnp.where(distance < half, distance, half + counted)


def contract_first(left, right):
    return lax.dot_general(
        left, right, (((0,), (0,)), ((), ())), preferred_element_type=jnp.float32
    )


def contract_last(left, right):
    return lax.dot_general(
        left, right, (((1,), (1,)), ((), ())), preferred_element_type=jnp.float32
    )


def plain(body, ins, outs, scratch=(), scalar=True):
    whole = pl.BlockSpec(memory_space=pltpu.VMEM)
    head = [pl.BlockSpec(memory_space=pltpu.SMEM)] if scalar else []
    return pl.pallas_call(
        body,
        out_shape=[jax.ShapeDtypeStruct(shape, dtype) for shape, dtype in outs],
        in_specs=head + [whole] * (len(ins) - len(head)),
        out_specs=[whole] * len(outs),
        scratch_shapes=list(scratch),
        compiler_params=pltpu.CompilerParams(vmem_limit_bytes=VMEM_LIMIT),
    )(*ins)


def mm(left, right):
    return jnp.dot(left, right, preferred_element_type=F32)


def join(ref):
    return jnp.concatenate([ref[s] for s in range(4)], axis=1)


def split(ref, value, share):
    for s in range(4):
        ref[s] = value[:, s * share : (s + 1) * share].astype(ref.dtype)


def valid_column(lengths, span):
    return (lax.broadcasted_iota(jnp.int32, (span, 1), 0) < lengths[0]).astype(F32)


def root(values):
    return lax.rsqrt(jnp.mean(values * values, axis=1, keepdims=True) + EPSILON)


def norm_back(values, gain, grad):
    scale = root(values)
    product = gain * grad
    inner = jnp.mean(product * values, axis=1, keepdims=True)
    gain_grad = jnp.sum(grad * values * scale, axis=0, keepdims=True)
    return scale * product - values * (scale * scale * scale) * inner, gain_grad


def attend_kernel(heads, lengths, tok, gain, wqkv, wout, bias, out, n1, qkv, prob, att):
    span, share = tok.shape[1], tok.shape[2]
    x = join(tok).astype(F32)
    normal = (x * root(x) * gain[...]).astype(BF)
    n1[...] = normal
    projected = mm(normal, wqkv[...]).astype(BF)
    row = lax.broadcasted_iota(jnp.int32, (span, span), 0)
    col = lax.broadcasted_iota(jnp.int32, (span, span), 1)
    allowed = (col <= row) & (col < lengths[0])
    parts = []
    for h in range(heads):
        q, k, v = (
            projected[:, m * share + h * HD : m * share + (h + 1) * HD] for m in range(3)
        )
        for m, value in enumerate((q, k, v)):
            qkv[m * heads + h] = value
        line = jnp.broadcast_to(bias[h : h + 1, :], (span, span))
        offsets = pltpu.roll(line, 0, 1, stride=1, stride_axis=0)
        scores = jnp.where(allowed, contract_last(q, k) * HD ** (-0.5) + offsets, -1000000000.0)
        powers = jnp.exp(scores - jnp.max(scores, axis=1, keepdims=True))
        p = powers / jnp.sum(powers, axis=1, keepdims=True)
        prob[h] = p
        parts.append(mm(p.astype(BF), v))
    attended = jnp.concatenate(parts, axis=1).astype(BF)
    att[...] = attended
    split(out, mm(attended, wout[...]) * valid_column(lengths, span), share)


def ranked(routes, experts):
    span = routes.shape[0]
    place = lax.broadcasted_iota(jnp.int32, (span, experts), 1)
    named = [(routes[:, k : k + 1] == place).astype(F32) for k in range(TOP)]
    row = lax.broadcasted_iota(jnp.int32, (span, span), 0)
    col = lax.broadcasted_iota(jnp.int32, (span, span), 1)
    before = mm((col < row).astype(F32).astype(BF), (named[0] + named[1]).astype(BF))
    return named, [jnp.sum(n * before, axis=1, keepdims=True).astype(jnp.int32) for n in named]


def placings(routes, experts, capacity):
    named, ranks = ranked(routes, experts)
    slots = lax.broadcasted_iota(jnp.int32, (routes.shape[0], experts * capacity), 1)
    placed = []
    for k in range(TOP):
        at = routes[:, k : k + 1] * capacity + ranks[k]
        placed.append((at == slots).astype(F32).astype(BF))
    return named, placed


def route_kernel(capacity, lengths, tok, att, gain, wrouter, routes, cot, out, n2, prob, gates):
    span, share = tok.shape[1], tok.shape[2]
    experts = wrouter.shape[1]
    me = lax.axis_index("shard")
    state = join(tok).astype(F32) + join(att).astype(F32)
    normal = (state * root(state) * gain[...]).astype(BF)
    split(n2, normal, share)
    logits = mm(normal, wrouter[...])
    powers = jnp.exp(logits - jnp.max(logits, axis=1, keepdims=True))
    p = powers / jnp.sum(powers, axis=1, keepdims=True)
    prob[...] = p
    named, placed = placings(routes[...], experts, capacity)
    picked = [jnp.sum(n * p, axis=1, keepdims=True) for n in named]
    both = picked[0] + picked[1]
    gate = [value / both for value in picked]
    for k in range(TOP):
        gates[:, k : k + 1] = gate[k]
    weighted = [value * valid_column(lengths, span) for value in gate]
    grad = cot[...].astype(F32)
    rows = contract_first(placed[0] + placed[1], n2[me]).astype(BF)
    grads = contract_first(placed[0], (weighted[0] * grad).astype(BF)) + contract_first(
        placed[1], (weighted[1] * grad).astype(BF)
    )
    grads = grads.astype(BF)
    for g in range(out.shape[0]):
        out[g, 0] = rows[g * capacity : (g + 1) * capacity]
        out[g, 1] = grads[g * capacity : (g + 1) * capacity]


def expert_kernel(x, w_in, w_out, out, g_in, g_out, rows, grads, hidden, pre_grads):
    groups, capacity, share = x.shape[1], x.shape[3], x.shape[4]
    count = groups // 2
    span = count * capacity
    factor = float(np.sqrt(2.0 / np.pi))
    for half in range(2):
        take = slice(half * count, (half + 1) * count)
        keep = slice(half * span, (half + 1) * span)

        def flat(kind):
            return jnp.concatenate(
                [x[s, take, kind].reshape(span, share) for s in range(4)], axis=1
            )

        value, grad = flat(0), flat(1)
        rows[keep] = value
        grads[keep] = grad
        pre = mm(value, w_in[...])
        t = jnp.tanh(factor * (pre + 0.044715 * pre * pre * pre))
        act = (0.5 * pre * (1.0 + t)).astype(BF)
        slope = 0.5 * (1.0 + t) + 0.5 * pre * (1.0 - t * t) * factor * (
            1.0 + 3 * 0.044715 * pre * pre
        )
        hidden[keep] = act
        y = mm(act, w_out[...]).astype(BF)
        pre_grad = (contract_last(grad, w_out[...]) * slope).astype(BF)
        pre_grads[keep] = pre_grad
        dx = contract_last(pre_grad, w_in[...]).astype(BF)
        for s in range(4):
            lanes = slice(s * share, (s + 1) * share)
            out[s, take, 0] = y[:, lanes].reshape(count, capacity, share)
            out[s, take, 1] = dx[:, lanes].reshape(count, capacity, share)
    for at in range(0, rows.shape[1], 256):
        g_in[at : at + 256] = contract_first(rows[:, at : at + 256], pre_grads[...])
    for at in range(0, hidden.shape[1], 256):
        g_out[at : at + 256] = contract_first(hidden[:, at : at + 256], grads[...])


def return_kernel(experts, lengths, got, routes, gates, cot, tok, att, out, n2share, gate_part):
    span, share = tok.shape[1], tok.shape[2]
    groups, capacity = got.shape[0], got.shape[2]
    me = lax.axis_index("shard")
    _, placed = placings(routes[...], experts, capacity)
    y = got[:, 0].reshape(groups * capacity, share)
    dx = got[:, 1].reshape(groups * capacity, share)
    valid = valid_column(lengths, span)
    grad = cot[...].astype(F32)
    mixture = jnp.zeros((span, share), F32)
    for k in range(TOP):
        picked = mm(placed[k], y)
        mixture = mixture + gates[:, k : k + 1] * picked
        gate_part[:, k : k + 1] = jnp.sum(grad * picked, axis=1, keepdims=True) * valid
    state = tok[me].astype(F32) + att[me].astype(F32)
    out[...] = (state + mixture * valid).astype(BF)
    n2share[...] = mm(placed[0] + placed[1], dx).astype(BF)


def back_kernel(
    heads, lengths, n2g, gate_grad, p_router, routes, n2, tok, att, gain, cot, wrouter, attended,
    wout, qkv, prob, n1, wqkv,
    sg_own, n1part, g_qkv, g_out, g_bias, g_gain, g_router, sg,
):
    span, share = tok.shape[1], tok.shape[2]
    experts = wrouter.shape[1]
    me = lax.axis_index("shard")
    valid = valid_column(lengths, span)
    p = p_router[...]
    place = lax.broadcasted_iota(jnp.int32, (span, experts), 1)
    named = [(routes[:, k : k + 1] == place).astype(F32) for k in range(TOP)]
    picked = [jnp.sum(n * p, axis=1, keepdims=True) for n in named]
    both = picked[0] + picked[1]
    dg = [gate_grad[:, k : k + 1] for k in range(TOP)]
    common = (dg[0] * picked[0] + dg[1] * picked[1]) / (both * both)
    dp = named[0] * (dg[0] / both - common) + named[1] * (dg[1] / both - common)
    dlogits = (p * (dp - jnp.sum(p * dp, axis=1, keepdims=True))).astype(BF)
    g_router[...] = contract_first(join(n2), dlogits)
    dn = join(n2g).astype(F32) + contract_last(dlogits, wrouter[...])
    state = join(tok).astype(F32) + join(att).astype(F32)
    dv, dgain = norm_back(state, gain[...], dn)
    g_gain[...] = dgain
    state_grad = join(cot).astype(F32) + dv
    split(sg, state_grad, share)
    sg_own[...] = sg[me]
    attn_grad = (state_grad * valid).astype(BF)
    g_out[...] = contract_first(attended[...], attn_grad).astype(BF)
    attended_grad = contract_last(attn_grad, wout[...]).astype(BF)
    row = lax.broadcasted_iota(jnp.int32, (span, span), 0)
    col = lax.broadcasted_iota(jnp.int32, (span, span), 1)
    flip = (row + col == span - 1).astype(F32).astype(BF)
    scale = HD ** (-0.5)
    dq, dk, dv_heads = [], [], []
    for h in range(heads):
        ag = attended_grad[:, h * HD : (h + 1) * HD]
        q, k, v = qkv[h], qkv[heads + h], qkv[2 * heads + h]
        w = prob[h]
        dprob = contract_last(ag, v)
        ds = (w * (dprob - jnp.sum(w * dprob, axis=1, keepdims=True))).astype(BF)
        dv_heads.append(contract_first(w.astype(BF), ag))
        dq.append(mm(ds, k) * scale)
        dk.append(contract_first(ds, q) * scale)
        lined = pltpu.roll(mm(flip, ds), 1, 1, stride=1, stride_axis=0)
        g_bias[h : h + 1, :] = jnp.sum(lined, axis=0, keepdims=True)
    projected = jnp.concatenate(dq + dk + dv_heads, axis=1).astype(BF)
    g_qkv[...] = contract_first(n1[...], projected).astype(BF)
    split(n1part, contract_last(projected, wqkv[...]), share)


def last_kernel(n1g, tok, gain, sg_own, out, g_gain, room):
    share = tok.shape[2]
    me = lax.axis_index("shard")
    dv, dgain = norm_back(join(tok).astype(F32), gain[...], join(n1g).astype(F32))
    g_gain[...] = dgain
    split(room, dv, share)
    out[...] = sg_own[...] + room[me]


def per_device(
    tokens,
    norm_gain1,
    qkv_weight,
    out_weight,
    rel_bias,
    norm_gain2,
    router_weight,
    in_weight,
    expert_out,
    lengths,
    routes,
    cotangent,
):
    span = tokens.shape[0]
    share = tokens.shape[1]
    width = qkv_weight.shape[0]
    heads = rel_bias.shape[0]
    groups = lax.axis_size("expert")
    experts = router_weight.shape[1]
    capacity = -(-(3 * span * TOP // (2 * experts)) // 16) * 16
    slots = experts * capacity
    columns = 3 * share
    blocks = (4, span, share)
    gain1, gain2 = norm_gain1[None], norm_gain2[None]
    distance = (span - jnp.arange(span, dtype=jnp.int32)) % span
    table_hot = (bucket_of(distance)[:, None] == jnp.arange(BUCKETS)[None, :]).astype(F32)
    bias = jnp.dot(rel_bias, table_hot.T, precision=lax.Precision.HIGHEST)
    token_blocks, grad_blocks = shard_gather([tokens, cotangent], 1)
    attn_part, normal_one, qkv, probability, attended = plain(
        functools.partial(attend_kernel, heads),
        [lengths, token_blocks, gain1, qkv_weight, out_weight, bias],
        [
            (blocks, BF),
            ((span, width), BF),
            ((3 * heads, span, HD), BF),
            ((heads, span, span), F32),
            ((span, share), BF),
        ],
    )
    attn_blocks = shard_sum(attn_part, 2)
    outgoing, normal_two, p_router, gates = plain(
        functools.partial(route_kernel, capacity),
        [lengths, token_blocks, attn_blocks, gain2, router_weight, routes, cotangent],
        [
            ((groups, 2, capacity, share), BF),
            (blocks, BF),
            ((span, experts), F32),
            ((span, TOP), F32),
        ],
    )
    incoming = dispatch(outgoing, 3)
    partials, grad_in_weight, grad_expert_out = plain(
        expert_kernel,
        [incoming, in_weight[0], expert_out[0]],
        [
            (incoming.shape, BF),
            (in_weight.shape[1:], F32),
            (expert_out.shape[1:], F32),
        ],
        [
            pltpu.VMEM((slots, width), BF),
            pltpu.VMEM((slots, width), BF),
            pltpu.VMEM((slots, in_weight.shape[2]), BF),
            pltpu.VMEM((slots, in_weight.shape[2]), BF),
        ],
        scalar=False,
    )
    returned = combine(partials, 4)
    output, normal_two_share, gate_part = plain(
        functools.partial(return_kernel, experts),
        [lengths, returned, routes, gates, cotangent, token_blocks, attn_blocks],
        [((span, share), BF), ((span, share), BF), ((span, TOP), F32)],
    )
    gate_rows = jnp.pad(gate_part.T, ((0, 8 - TOP), (0, 0)))
    normal_two_blocks, gate_blocks = shard_gather([normal_two_share, gate_rows], 5)
    gate_grad = jnp.sum(gate_blocks, axis=0)[:TOP].T
    state_grad_own, normal_one_part, grad_qkv, grad_out, grad_bias, grad_gain2, grad_router = plain(
        functools.partial(back_kernel, heads),
        [
            lengths, normal_two_blocks, gate_grad, p_router, routes, normal_two, token_blocks,
            attn_blocks, gain2, grad_blocks, router_weight, attended, out_weight, qkv,
            probability, normal_one, qkv_weight,
        ],
        [
            ((span, share), F32),
            (blocks, BF),
            ((width, columns), BF),
            ((share, width), BF),
            ((heads, span), F32),
            ((1, width), F32),
            ((width, experts), F32),
        ],
        [pltpu.VMEM(blocks, F32)],
    )
    grad_rel_bias = jnp.dot(grad_bias, table_hot, precision=lax.Precision.HIGHEST)
    normal_one_blocks = shard_sum(normal_one_part, 6)
    token_grad, grad_gain1 = plain(
        last_kernel,
        [normal_one_blocks, token_blocks, gain1, state_grad_own],
        [((span, share), F32), ((1, width), F32)],
        [pltpu.VMEM(blocks, F32)],
        scalar=False,
    )
    small_parts = [grad_rel_bias, grad_gain1, grad_gain2, grad_router]
    small = jnp.concatenate([part.reshape(-1) for part in small_parts])
    small_rows = -(-small.shape[0] // (groups * 1024)) * 8
    small = jnp.pad(small, (0, groups * small_rows * 128 - small.shape[0]))
    lines = groups // 2
    grad_qkv, grad_out, small = expert_sum(
        [
            grad_qkv.reshape(2, lines, -1, columns),
            grad_out.reshape(2, lines, -1, width if share % (16 * groups) == 0 else share),
            small.reshape(2, lines, small_rows, 128),
        ],
        7,
    )
    small = small.reshape(-1)
    summed, start = [], 0
    for part in small_parts:
        summed.append(small[start : start + part.size].reshape(part.shape))
        start += part.size
    return (
        output,
        token_grad,
        summed[1][0],
        grad_qkv.reshape(width, columns).astype(F32),
        grad_out.reshape(share, width).astype(F32),
        summed[0],
        summed[2][0],
        summed[3],
        grad_in_weight[None],
        grad_expert_out[None],
    )


def solution(mesh):
    placed = (
        P("expert", "shard"),
        P(),
        P(None, "shard"),
        P("shard", None),
        P("shard", None),
        P(),
        P(),
        P("expert", None, "shard"),
        P("expert", "shard", None),
        P("expert"),
        P("expert", None),
        P("expert", "shard"),
    )
    return jax.shard_map(
        per_device,
        mesh=mesh,
        in_specs=placed,
        out_specs=(
            P("expert", "shard"),
            P("expert", "shard"),
            P(),
            P(None, "shard"),
            P("shard", None),
            P("shard", None),
            P(),
            P(),
            P("expert", None, "shard"),
            P("expert", "shard", None),
        ),
        check_vma=False,
    )
```

```python
import functools

import jax
import jax.numpy as jnp
import numpy as np
from jax import lax
from jax.experimental import pallas as pl
from jax.experimental.pallas import tpu as pltpu
from jax.sharding import PartitionSpec as P

HD = 64
TOP = 2
BUCKETS = 32
MAX_DIST = 128


EPSILON = 1e-06
MESH = pl.DeviceIdType.MESH
VMEM_LIMIT = 40 * 1024 * 1024
BF = jnp.bfloat16
F32 = jnp.float32


def remote(src, dst, send_sem, recv_sem, **where):
    return pltpu.make_async_remote_copy(
        src_ref=src,
        dst_ref=dst,
        send_sem=send_sem,
        recv_sem=recv_sem,
        device_id=where,
        device_id_type=MESH,
    )


def shard_peers():
    me = lax.axis_index("shard")
    near = me + 1 - 2 * lax.rem(me, 2)
    far = lax.rem(me + 2, 4)
    cross = lax.rem(near + 2, 4)
    return me, near, far, cross


def greet_shard(extra=0):
    barrier = pltpu.get_barrier_semaphore()
    _, near, far, _ = shard_peers()
    pl.semaphore_signal(barrier, inc=1, device_id={"shard": near}, device_id_type=MESH)
    pl.semaphore_signal(barrier, inc=1, device_id={"shard": far}, device_id_type=MESH)
    pl.semaphore_wait(barrier, 2 + extra)


def greet_expert(groups):
    barrier = pltpu.get_barrier_semaphore()
    here = lax.axis_index("expert")

    def greet(step, carry):
        pl.semaphore_signal(
            barrier, inc=1, device_id={"expert": lax.rem(here + step, groups)}, device_id_type=MESH
        )
        return carry

    lax.fori_loop(1, groups, greet, 0)


def loop(start, stop, body):
    def run(step, carry):
        body(step)
        return carry

    lax.fori_loop(start, stop, run, 0)


def call_kernel(body, ins, outs, scratch, collective):
    return pl.pallas_call(
        body,
        out_shape=outs,
        in_specs=[pl.BlockSpec(memory_space=pltpu.VMEM)] * len(ins),
        out_specs=[pl.BlockSpec(memory_space=pltpu.VMEM)] * len(outs),
        scratch_shapes=scratch,
        compiler_params=pltpu.CompilerParams(
            collective_id=collective, has_side_effects=True, vmem_limit_bytes=VMEM_LIMIT
        ),
    )(*ins)


def gather_kernel(count, *refs):
    ins, outs = refs[:count], refs[count : 2 * count]
    send, recv = refs[2 * count :]
    me, near, far, cross = shard_peers()
    greet_shard()
    first, second = [], []
    for i in range(count):
        one = remote(ins[i], outs[i].at[me], send.at[i, 0], recv.at[i, 0], shard=far)
        two = remote(ins[i], outs[i].at[me], send.at[i, 1], recv.at[i, 1], shard=near)
        one.start()
        two.start()
        first.append(one)
        second.append(two)
    for i in range(count):
        outs[i][me] = ins[i][...]
    for i in range(count):
        first[i].wait_recv()
        passed = remote(
            outs[i].at[far], outs[i].at[far], send.at[i, 2], recv.at[i, 2], shard=near
        )
        passed.start()
        second.append(passed)
    for i in range(count):
        first[i].wait_send()
    for copy in second:
        copy.wait()


def shard_gather(arrays, collective):
    count = len(arrays)
    return call_kernel(
        functools.partial(gather_kernel, count),
        arrays,
        [jax.ShapeDtypeStruct((4,) + a.shape, a.dtype) for a in arrays],
        [pltpu.SemaphoreType.DMA((count, 3)), pltpu.SemaphoreType.DMA((count, 3))],
        collective,
    )


def sum_kernel(x, out, got, mid, last, send, recv):
    me, near, far, cross = shard_peers()
    greet_shard()
    one = remote(x.at[cross], got.at[1], send.at[0], recv.at[0], shard=near)
    two = remote(x.at[near], got.at[0], send.at[1], recv.at[1], shard=near)
    one.start()
    two.start()
    one.wait_recv()
    mid[...] = (x[far].astype(F32) + got[1].astype(F32)).astype(BF)
    three = remote(mid, last, send.at[2], recv.at[2], shard=far)
    three.start()
    two.wait_recv()
    three.wait_recv()
    out[me] = (x[me].astype(F32) + got[0].astype(F32) + last[...].astype(F32)).astype(BF)
    four = remote(out.at[me], out.at[me], send.at[3], recv.at[3], shard=far)
    five = remote(out.at[me], out.at[me], send.at[4], recv.at[4], shard=near)
    four.start()
    five.start()
    four.wait_recv()
    six = remote(out.at[far], out.at[far], send.at[5], recv.at[5], shard=near)
    six.start()
    five.wait_recv()
    six.wait_recv()
    for copy in (one, two, three, four, five, six):
        copy.wait_send()


def shard_sum(blocks, collective):
    _, rows, columns = blocks.shape
    return call_kernel(
        sum_kernel,
        [blocks],
        [jax.ShapeDtypeStruct(blocks.shape, BF)],
        [
            pltpu.VMEM((2, rows, columns), BF),
            pltpu.VMEM((rows, columns), BF),
            pltpu.VMEM((rows, columns), BF),
            pltpu.SemaphoreType.DMA((6,)),
            pltpu.SemaphoreType.DMA((6,)),
        ],
        collective,
    )[0]


def dispatch_kernel(groups, x, out, s0, r0, s1, r1, s2, r2, s3, r3):
    here = lax.axis_index("expert")
    me, near, far, cross = shard_peers()
    greet_expert(groups)
    greet_shard(groups - 1)

    def origin(step):
        return lax.rem(here + groups - step, groups)

    def sent(step):
        there = lax.rem(here + step, groups)
        return remote(x.at[there], out.at[me, here], s0.at[step], r0.at[step], expert=there)

    def block(step, place, send, recv, peer):
        at = origin(step)
        return remote(
            out.at[place, at], out.at[place, at], send.at[step], recv.at[step], shard=peer
        )

    def spread(step):
        block(step, me, s2, r2, far).start()
        block(step, me, s1, r1, near).start()

    def passed(step):
        block(step, far, s2, r2, far).wait_recv()
        block(step, far, s3, r3, near).start()

    loop(1, groups, lambda step: sent(step).start())
    out[me, here] = x[here]
    spread(0)

    def middle(step):
        at = origin(step)
        remote(x.at[at], out.at[me, at], s0.at[step], r0.at[step], expert=at).wait_recv()
        spread(step)
        passed(step - 1)

    loop(1, groups, middle)
    passed(groups - 1)

    def finish(step):
        block(step, near, s1, r1, near).wait_recv()
        block(step, cross, s3, r3, near).wait_recv()
        block(step, me, s1, r1, near).wait_send()
        block(step, me, s2, r2, far).wait_send()
        block(step, far, s3, r3, near).wait_send()

    loop(0, groups, finish)
    loop(1, groups, lambda step: sent(step).wait_send())


def dispatch(blocks, collective):
    groups = blocks.shape[0]
    return call_kernel(
        functools.partial(dispatch_kernel, groups),
        [blocks],
        [jax.ShapeDtypeStruct((4,) + blocks.shape, BF)],
        [pltpu.SemaphoreType.DMA((groups,))] * 8,
        collective,
    )[0]


def combine_kernel(groups, x, out, got, mid, last, done, s0, r0, s1, r1, s2, r2, s3, r3):
    here = lax.axis_index("expert")
    me, near, far, cross = shard_peers()
    greet_expert(groups)
    greet_shard(groups - 1)

    def place(step):
        return lax.rem(here + 1 + step, groups)

    def first(step):
        at = place(step)
        return remote(x.at[cross, at], got.at[1, at], s0.at[step], r0.at[step], shard=near)

    def second(step):
        at = place(step)
        return remote(x.at[near, at], got.at[0, at], s1.at[step], r1.at[step], shard=near)

    def third(step):
        at = place(step)
        return remote(mid.at[at], last.at[at], s2.at[step], r2.at[step], shard=far)

    def home(step):
        at = place(step)
        return remote(done.at[at], out.at[here], s3.at[step], r3.at[step], expert=at)

    def begin(step):
        first(step).start()
        second(step).start()

    def half(step):
        at = place(step)
        first(step).wait_recv()
        mid[at] = (x[far, at].astype(F32) + got[1, at].astype(F32)).astype(BF)
        third(step).start()

    def whole(step):
        at = place(step)
        second(step).wait_recv()
        third(step).wait_recv()
        return (
            x[me, at].astype(F32) + got[0, at].astype(F32) + last[at].astype(F32)
        ).astype(BF)

    def back(step):
        done[place(step)] = whole(step)
        home(step).start()

    loop(0, groups, begin)
    half(0)

    def middle(step):
        half(step)
        back(step - 1)

    loop(1, groups, middle)
    out[here] = whole(groups - 1)

    def finish(step):
        source = lax.rem(here + groups - 1 - step, groups)
        remote(
            done.at[source], out.at[source], s3.at[step], r3.at[step], expert=source
        ).wait_recv()
        home(step).wait_send()

    loop(0, groups - 1, finish)

    def sent(step):
        first(step).wait_send()
        second(step).wait_send()
        third(step).wait_send()

    loop(0, groups, sent)


def combine(blocks, collective):
    groups = blocks.shape[1]
    shape = blocks.shape[1:]
    return call_kernel(
        functools.partial(combine_kernel, groups),
        [blocks],
        [jax.ShapeDtypeStruct(shape, BF)],
        [
            pltpu.VMEM((2,) + shape, BF),
            pltpu.VMEM(shape, BF),
            pltpu.VMEM(shape, BF),
            pltpu.VMEM(shape, BF),
        ]
        + [pltpu.SemaphoreType.DMA((groups,))] * 8,
        collective,
    )[0]


def total_kernel(count, lines, *refs):
    ins, outs = refs[:count], refs[count : 2 * count]
    got, mid, parts = (refs[(2 + i) * count : (3 + i) * count] for i in range(3))
    sa, ra, sb, rb, sc, rc, sd, rd = refs[5 * count :]
    here = lax.axis_index("expert")
    side = lax.rem(here, 2)
    line = here // 2
    partner = here + 1 - 2 * side
    other = 1 - side
    barrier = pltpu.get_barrier_semaphore()
    pl.semaphore_signal(barrier, inc=1, device_id={"expert": partner}, device_id_type=MESH)

    def on_line(step):
        return lax.rem(line + step, lines)

    def from_line(step):
        return lax.rem(line + lines - step, lines)

    def greet(step):
        pl.semaphore_signal(
            barrier, inc=1, device_id={"expert": 2 * on_line(step) + side}, device_id_type=MESH
        )

    loop(1, lines, greet)
    pl.semaphore_wait(barrier, lines)

    def cross(i, step):
        at = on_line(step)
        return remote(
            ins[i].at[other, at], got[i].at[at], sa.at[i, step], ra.at[i, step], expert=partner
        )

    def along(i, step, at):
        return remote(
            mid[i].at[at], parts[i].at[line], sb.at[i, step], rb.at[i, step],
            expert=2 * at + side,
        )

    def arrive(i, step):
        at = from_line(step)
        return remote(
            mid[i].at[at], parts[i].at[at], sb.at[i, step], rb.at[i, step], expert=2 * at + side
        )

    def result(i, step):
        at = on_line(step)
        return remote(
            outs[i].at[side, line], outs[i].at[side, line], sc.at[i, step], rc.at[i, step],
            expert=2 * at + side,
        )

    def landed(i, step):
        at = from_line(step)
        return remote(
            outs[i].at[side, at], outs[i].at[side, at], sc.at[i, step], rc.at[i, step],
            expert=2 * at + side,
        )

    def shared(i, step, where):
        at = from_line(step)
        return remote(
            outs[i].at[where, at], outs[i].at[where, at], sd.at[i, step], rd.at[i, step],
            expert=partner,
        )

    def crossing(step):
        for i in range(count):
            cross(i, step).start()

    loop(1, lines, crossing)
    crossing(0)

    def paired(step):
        at = on_line(step)
        for i in range(count):
            cross(i, step).wait_recv()
            mid[i][at] = (ins[i][side, at].astype(F32) + got[i][at].astype(F32)).astype(
                ins[i].dtype
            )
            along(i, step, at).start()

    loop(1, lines, paired)
    for i in range(count):
        cross(i, 0).wait_recv()
        parts[i][line] = (ins[i][side, line].astype(F32) + got[i][line].astype(F32)).astype(
            ins[i].dtype
        )

    def arrived(step):
        for i in range(count):
            arrive(i, step).wait_recv()

    loop(1, lines, arrived)
    for i in range(count):
        added = parts[i][0].astype(F32)
        for at in range(1, lines):
            added = added + parts[i][at].astype(F32)
        outs[i][side, line] = added.astype(ins[i].dtype)

    def publish(step):
        for i in range(count):
            result(i, step).start()

    loop(1, lines, publish)
    for i in range(count):
        shared(i, 0, side).start()

    def relay(step):
        for i in range(count):
            landed(i, step).wait_recv()
            shared(i, step, side).start()

    loop(1, lines, relay)

    def finish(step):
        for i in range(count):
            shared(i, step, other).wait_recv()
            shared(i, step, side).wait_send()
            cross(i, step).wait_send()

    loop(0, lines, finish)

    def sent(step):
        for i in range(count):
            along(i, step, on_line(step)).wait_send()
            result(i, step).wait_send()

    loop(1, lines, sent)


def expert_sum(arrays, collective):
    count, lines = len(arrays), arrays[0].shape[1]
    room = [pltpu.VMEM(a.shape[1:], a.dtype) for a in arrays]
    return call_kernel(
        functools.partial(total_kernel, count, lines),
        arrays,
        [jax.ShapeDtypeStruct(a.shape, a.dtype) for a in arrays],
        room * 3 + [pltpu.SemaphoreType.DMA((count, lines))] * 8,
        collective,
    )


def bucket_of(distance):
    half = BUCKETS // 2
    powers = np.arange(1, half)
    edges = np.ceil(half * (MAX_DIST / half) ** (powers / half))
    counted = jnp.zeros(distance.shape, jnp.int32)
    for threshold in edges:
        counted = counted + (distance >= int(threshold)).astype(jnp.int32)
    return jnp.where(distance < half, distance, half + counted)


def contract_first(left, right):
    return lax.dot_general(
        left, right, (((0,), (0,)), ((), ())), preferred_element_type=jnp.float32
    )


def contract_last(left, right):
    return lax.dot_general(
        left, right, (((1,), (1,)), ((), ())), preferred_element_type=jnp.float32
    )


def plain(body, ins, outs, scratch=(), scalar=True):
    whole = pl.BlockSpec(memory_space=pltpu.VMEM)
    head = [pl.BlockSpec(memory_space=pltpu.SMEM)] if scalar else []
    return pl.pallas_call(
        body,
        out_shape=[jax.ShapeDtypeStruct(shape, dtype) for shape, dtype in outs],
        in_specs=head + [whole] * (len(ins) - len(head)),
        out_specs=[whole] * len(outs),
        scratch_shapes=list(scratch),
        compiler_params=pltpu.CompilerParams(vmem_limit_bytes=VMEM_LIMIT),
    )(*ins)


def mm(left, right):
    return jnp.dot(left, right, preferred_element_type=F32)


def join(ref):
    return jnp.concatenate([ref[s] for s in range(4)], axis=1)


def split(ref, value, share):
    for s in range(4):
        ref[s] = value[:, s * share : (s + 1) * share].astype(ref.dtype)


def valid_column(lengths, span):
    return (lax.broadcasted_iota(jnp.int32, (span, 1), 0) < lengths[0]).astype(F32)


def root(values):
    return lax.rsqrt(jnp.mean(values * values, axis=1, keepdims=True) + EPSILON)


def norm_back(values, gain, grad):
    scale = root(values)
    product = gain * grad
    inner = jnp.mean(product * values, axis=1, keepdims=True)
    gain_grad = jnp.sum(grad * values * scale, axis=0, keepdims=True)
    return scale * product - values * (scale * scale * scale) * inner, gain_grad


def attend_kernel(heads, lengths, tok, gain, wqkv, wout, bias, out, n1, qkv, prob, att):
    span, share = tok.shape[1], tok.shape[2]
    x = join(tok).astype(F32)
    normal = (x * root(x) * gain[...]).astype(BF)
    n1[...] = normal
    projected = mm(normal, wqkv[...]).astype(BF)
    row = lax.broadcasted_iota(jnp.int32, (span, span), 0)
    col = lax.broadcasted_iota(jnp.int32, (span, span), 1)
    allowed = (col <= row) & (col < lengths[0])
    parts = []
    for h in range(heads):
        q, k, v = (
            projected[:, m * share + h * HD : m * share + (h + 1) * HD] for m in range(3)
        )
        for m, value in enumerate((q, k, v)):
            qkv[m * heads + h] = value
        line = jnp.broadcast_to(bias[h : h + 1, :], (span, span))
        offsets = pltpu.roll(line, 0, 1, stride=1, stride_axis=0)
        scores = jnp.where(allowed, contract_last(q, k) * HD ** (-0.5) + offsets, -1000000000.0)
        powers = jnp.exp(scores - jnp.max(scores, axis=1, keepdims=True))
        p = powers / jnp.sum(powers, axis=1, keepdims=True)
        prob[h] = p
        parts.append(mm(p.astype(BF), v))
    attended = jnp.concatenate(parts, axis=1).astype(BF)
    att[...] = attended
    split(out, mm(attended, wout[...]) * valid_column(lengths, span), share)


def ranked(routes, experts):
    span = routes.shape[0]
    place = lax.broadcasted_iota(jnp.int32, (span, experts), 1)
    named = [(routes[:, k : k + 1] == place).astype(F32) for k in range(TOP)]
    row = lax.broadcasted_iota(jnp.int32, (span, span), 0)
    col = lax.broadcasted_iota(jnp.int32, (span, span), 1)
    before = mm((col < row).astype(F32).astype(BF), (named[0] + named[1]).astype(BF))
    return named, [jnp.sum(n * before, axis=1, keepdims=True).astype(jnp.int32) for n in named]


def placings(routes, experts, capacity):
    named, ranks = ranked(routes, experts)
    slots = lax.broadcasted_iota(jnp.int32, (routes.shape[0], experts * capacity), 1)
    placed = []
    for k in range(TOP):
        at = routes[:, k : k + 1] * capacity + ranks[k]
        placed.append((at == slots).astype(F32).astype(BF))
    return named, placed


def route_kernel(capacity, lengths, tok, att, gain, wrouter, routes, cot, out, n2, prob, gates):
    span, share = tok.shape[1], tok.shape[2]
    experts = wrouter.shape[1]
    me = lax.axis_index("shard")
    state = join(tok).astype(F32) + join(att).astype(F32)
    normal = (state * root(state) * gain[...]).astype(BF)
    split(n2, normal, share)
    logits = mm(normal, wrouter[...])
    powers = jnp.exp(logits - jnp.max(logits, axis=1, keepdims=True))
    p = powers / jnp.sum(powers, axis=1, keepdims=True)
    prob[...] = p
    named, placed = placings(routes[...], experts, capacity)
    picked = [jnp.sum(n * p, axis=1, keepdims=True) for n in named]
    both = picked[0] + picked[1]
    gate = [value / both for value in picked]
    for k in range(TOP):
        gates[:, k : k + 1] = gate[k]
    weighted = [value * valid_column(lengths, span) for value in gate]
    grad = cot[...].astype(F32)
    rows = contract_first(placed[0] + placed[1], n2[me]).astype(BF)
    grads = contract_first(placed[0], (weighted[0] * grad).astype(BF)) + contract_first(
        placed[1], (weighted[1] * grad).astype(BF)
    )
    packed = jnp.concatenate([rows, grads.astype(BF)], axis=1)
    for g in range(out.shape[0]):
        out[g] = packed[g * capacity : (g + 1) * capacity]


def expert_kernel(x, w_in, w_out, out, g_in, g_out, rows, grads, hidden, pre_grads):
    groups, capacity, share = x.shape[1], x.shape[2], x.shape[3] // 2
    count = groups // 2
    span = count * capacity
    factor = float(np.sqrt(2.0 / np.pi))
    for half in range(2):
        take = slice(half * count, (half + 1) * count)
        keep = slice(half * span, (half + 1) * span)

        def flat(kind):
            lanes = slice(kind * share, (kind + 1) * share)
            return jnp.concatenate(
                [x[s, take].reshape(span, 2 * share)[:, lanes] for s in range(4)], axis=1
            )

        value, grad = flat(0), flat(1)
        rows[keep] = value
        grads[keep] = grad
        pre = mm(value, w_in[...])
        t = jnp.tanh(factor * (pre + 0.044715 * pre * pre * pre))
        act = (0.5 * pre * (1.0 + t)).astype(BF)
        slope = 0.5 * (1.0 + t) + 0.5 * pre * (1.0 - t * t) * factor * (
            1.0 + 3 * 0.044715 * pre * pre
        )
        hidden[keep] = act
        y = mm(act, w_out[...]).astype(BF)
        pre_grad = (contract_last(grad, w_out[...]) * slope).astype(BF)
        pre_grads[keep] = pre_grad
        dx = contract_last(pre_grad, w_in[...]).astype(BF)
        for s in range(4):
            lanes = slice(s * share, (s + 1) * share)
            both = jnp.concatenate([y[:, lanes], dx[:, lanes]], axis=1)
            out[s, take] = both.reshape(count, capacity, 2 * share)
    for at in range(0, rows.shape[1], 256):
        g_in[at : at + 256] = contract_first(rows[:, at : at + 256], pre_grads[...])
    for at in range(0, hidden.shape[1], 256):
        g_out[at : at + 256] = contract_first(hidden[:, at : at + 256], grads[...])


def return_kernel(experts, lengths, got, routes, gates, cot, tok, att, out, n2share, gate_part):
    span, share = tok.shape[1], tok.shape[2]
    groups, capacity = got.shape[0], got.shape[1]
    me = lax.axis_index("shard")
    _, placed = placings(routes[...], experts, capacity)
    both = got[...].reshape(groups * capacity, 2 * share)
    y, dx = both[:, :share], both[:, share:]
    valid = valid_column(lengths, span)
    grad = cot[...].astype(F32)
    mixture = jnp.zeros((span, share), F32)
    for k in range(TOP):
        picked = mm(placed[k], y)
        mixture = mixture + gates[:, k : k + 1] * picked
        gate_part[:, k : k + 1] = jnp.sum(grad * picked, axis=1, keepdims=True) * valid
    state = tok[me].astype(F32) + att[me].astype(F32)
    out[...] = (state + mixture * valid).astype(BF)
    n2share[...] = mm(placed[0] + placed[1], dx).astype(BF)


def back_kernel(
    heads, lengths, n2g, gate_grad, p_router, routes, n2, tok, att, gain, cot, wrouter, attended,
    wout, qkv, prob, n1, wqkv,
    sg_own, n1part, dense, g_bias, g_gain, g_router, sg,
):
    span, share = tok.shape[1], tok.shape[2]
    experts = wrouter.shape[1]
    me = lax.axis_index("shard")
    valid = valid_column(lengths, span)
    p = p_router[...]
    place = lax.broadcasted_iota(jnp.int32, (span, experts), 1)
    named = [(routes[:, k : k + 1] == place).astype(F32) for k in range(TOP)]
    picked = [jnp.sum(n * p, axis=1, keepdims=True) for n in named]
    both = picked[0] + picked[1]
    dg = [gate_grad[:, k : k + 1] for k in range(TOP)]
    common = (dg[0] * picked[0] + dg[1] * picked[1]) / (both * both)
    dp = named[0] * (dg[0] / both - common) + named[1] * (dg[1] / both - common)
    dlogits = (p * (dp - jnp.sum(p * dp, axis=1, keepdims=True))).astype(BF)
    g_router[...] = contract_first(join(n2), dlogits)
    dn = join(n2g).astype(F32) + contract_last(dlogits, wrouter[...])
    state = join(tok).astype(F32) + join(att).astype(F32)
    dv, dgain = norm_back(state, gain[...], dn)
    g_gain[...] = dgain
    state_grad = join(cot).astype(F32) + dv
    split(sg, state_grad, share)
    sg_own[...] = sg[me]
    attn_grad = (state_grad * valid).astype(BF)
    g_out = contract_first(attended[...], attn_grad).astype(BF)
    attended_grad = contract_last(attn_grad, wout[...]).astype(BF)
    row = lax.broadcasted_iota(jnp.int32, (span, span), 0)
    col = lax.broadcasted_iota(jnp.int32, (span, span), 1)
    flip = (row + col == span - 1).astype(F32).astype(BF)
    scale = HD ** (-0.5)
    dq, dk, dv_heads = [], [], []
    for h in range(heads):
        ag = attended_grad[:, h * HD : (h + 1) * HD]
        q, k, v = qkv[h], qkv[heads + h], qkv[2 * heads + h]
        w = prob[h]
        dprob = contract_last(ag, v)
        ds = (w * (dprob - jnp.sum(w * dprob, axis=1, keepdims=True))).astype(BF)
        dv_heads.append(contract_first(w.astype(BF), ag))
        dq.append(mm(ds, k) * scale)
        dk.append(contract_first(ds, q) * scale)
        lined = pltpu.roll(mm(flip, ds), 1, 1, stride=1, stride_axis=0)
        g_bias[h : h + 1, :] = jnp.sum(lined, axis=0, keepdims=True)
    projected = jnp.concatenate(dq + dk + dv_heads, axis=1).astype(BF)
    g_qkv = contract_first(n1[...], projected).astype(BF)
    stacked = jnp.concatenate([g_out[:, s * share : (s + 1) * share] for s in range(4)], axis=0)
    dense[...] = jnp.concatenate([g_qkv, stacked], axis=1)
    split(n1part, contract_last(projected, wqkv[...]), share)


def last_kernel(n1g, tok, gain, sg_own, out, g_gain, room):
    share = tok.shape[2]
    me = lax.axis_index("shard")
    dv, dgain = norm_back(join(tok).astype(F32), gain[...], join(n1g).astype(F32))
    g_gain[...] = dgain
    split(room, dv, share)
    out[...] = sg_own[...] + room[me]


def per_device(
    tokens,
    norm_gain1,
    qkv_weight,
    out_weight,
    rel_bias,
    norm_gain2,
    router_weight,
    in_weight,
    expert_out,
    lengths,
    routes,
    cotangent,
):
    span = tokens.shape[0]
    share = tokens.shape[1]
    width = qkv_weight.shape[0]
    heads = rel_bias.shape[0]
    groups = lax.axis_size("expert")
    experts = router_weight.shape[1]
    capacity = -(-(3 * span * TOP // (2 * experts)) // 16) * 16
    slots = experts * capacity
    columns = 3 * share
    blocks = (4, span, share)
    gain1, gain2 = norm_gain1[None], norm_gain2[None]
    distance = (span - jnp.arange(span, dtype=jnp.int32)) % span
    table_hot = (bucket_of(distance)[:, None] == jnp.arange(BUCKETS)[None, :]).astype(F32)
    bias = jnp.dot(rel_bias, table_hot.T, precision=lax.Precision.HIGHEST)
    token_blocks, grad_blocks = shard_gather([tokens, cotangent], 1)
    attn_part, normal_one, qkv, probability, attended = plain(
        functools.partial(attend_kernel, heads),
        [lengths, token_blocks, gain1, qkv_weight, out_weight, bias],
        [
            (blocks, BF),
            ((span, width), BF),
            ((3 * heads, span, HD), BF),
            ((heads, span, span), F32),
            ((span, share), BF),
        ],
    )
    attn_blocks = shard_sum(attn_part, 2)
    outgoing, normal_two, p_router, gates = plain(
        functools.partial(route_kernel, capacity),
        [lengths, token_blocks, attn_blocks, gain2, router_weight, routes, cotangent],
        [
            ((groups, capacity, 2 * share), BF),
            (blocks, BF),
            ((span, experts), F32),
            ((span, TOP), F32),
        ],
    )
    incoming = dispatch(outgoing, 3)
    partials, grad_in_weight, grad_expert_out = plain(
        expert_kernel,
        [incoming, in_weight[0], expert_out[0]],
        [
            (incoming.shape, BF),
            (in_weight.shape[1:], F32),
            (expert_out.shape[1:], F32),
        ],
        [
            pltpu.VMEM((slots, width), BF),
            pltpu.VMEM((slots, width), BF),
            pltpu.VMEM((slots, in_weight.shape[2]), BF),
            pltpu.VMEM((slots, in_weight.shape[2]), BF),
        ],
        scalar=False,
    )
    returned = combine(partials, 4)
    output, normal_two_share, gate_part = plain(
        functools.partial(return_kernel, experts),
        [lengths, returned, routes, gates, cotangent, token_blocks, attn_blocks],
        [((span, share), BF), ((span, share), BF), ((span, TOP), F32)],
    )
    gate_rows = jnp.pad(gate_part.T, ((0, 8 - TOP), (0, 0)))
    normal_two_blocks, gate_blocks = shard_gather([normal_two_share, gate_rows], 5)
    gate_grad = jnp.sum(gate_blocks, axis=0)[:TOP].T
    state_grad_own, normal_one_part, dense, grad_bias, grad_gain2, grad_router = plain(
        functools.partial(back_kernel, heads),
        [
            lengths, normal_two_blocks, gate_grad, p_router, routes, normal_two, token_blocks,
            attn_blocks, gain2, grad_blocks, router_weight, attended, out_weight, qkv,
            probability, normal_one, qkv_weight,
        ],
        [
            ((span, share), F32),
            (blocks, BF),
            ((width, width), BF),
            ((heads, span), F32),
            ((1, width), F32),
            ((width, experts), F32),
        ],
        [pltpu.VMEM(blocks, F32)],
    )
    grad_rel_bias = jnp.dot(grad_bias, table_hot, precision=lax.Precision.HIGHEST)
    normal_one_blocks = shard_sum(normal_one_part, 6)
    token_grad, grad_gain1 = plain(
        last_kernel,
        [normal_one_blocks, token_blocks, gain1, state_grad_own],
        [((span, share), F32), ((1, width), F32)],
        [pltpu.VMEM(blocks, F32)],
        scalar=False,
    )
    small_parts = [grad_rel_bias, grad_gain1, grad_gain2, grad_router]
    small = jnp.concatenate([part.reshape(-1) for part in small_parts])
    small_rows = -(-small.shape[0] // (groups * 1024)) * 8
    small = jnp.pad(small, (0, groups * small_rows * 128 - small.shape[0]))
    lines = groups // 2
    dense, small = expert_sum(
        [
            dense.reshape(2, lines, -1, width),
            small.reshape(2, lines, small_rows, 128),
        ],
        7,
    )
    dense = dense.reshape(width, width)
    grad_out = dense[:, columns:].reshape(4, share, share).transpose(1, 0, 2)
    small = small.reshape(-1)
    summed, start = [], 0
    for part in small_parts:
        summed.append(small[start : start + part.size].reshape(part.shape))
        start += part.size
    return (
        output,
        token_grad,
        summed[1][0],
        dense[:, :columns].astype(F32),
        grad_out.reshape(share, width).astype(F32),
        summed[0],
        summed[2][0],
        summed[3],
        grad_in_weight[None],
        grad_expert_out[None],
    )


def solution(mesh):
    placed = (
        P("expert", "shard"),
        P(),
        P(None, "shard"),
        P("shard", None),
        P("shard", None),
        P(),
        P(),
        P("expert", None, "shard"),
        P("expert", "shard", None),
        P("expert"),
        P("expert", None),
        P("expert", "shard"),
    )
    return jax.shard_map(
        per_device,
        mesh=mesh,
        in_specs=placed,
        out_specs=(
            P("expert", "shard"),
            P("expert", "shard"),
            P(),
            P(None, "shard"),
            P("shard", None),
            P("shard", None),
            P(),
            P(),
            P("expert", None, "shard"),
            P("expert", "shard", None),
        ),
        check_vma=False,
    )
```
